256 devices in a mesh: tile: 32 (over y, z), vir: 8 (over x, core).
Axes of the slice: x: 4, y: 4, z: 8, core: 2. Of those that a mesh axis runs over, the one named last changes fastest.
Arguments:
- amplitudes: bfloat16 [2048, 128, 512], P('vir', 'tile'), may hold values from -6 to 6
- source_block: bfloat16 [2048, 128, 512], P('vir', 'tile'), may hold values from -4 to 4
- ladder_integrals: bfloat16 [2048, 2048], P('vir'), may hold values from -0.110485435 to 0.110485435, as said below
- cholesky_vectors: bfloat16 [2048, 128, 1024], P('vir', 'tile'), may hold values from -0.0625 to 0.0625
- integral_tiles: int32 [32, 32], replicated, may hold values from 0 to 1, as said below
- amplitude_tiles: int32 [32, 128], replicated, may hold values 0 or 1
Outputs:
- residual: bfloat16 [2048, 128, 512], P('vir', 'tile')
The draws below stay inside these ranges and needn't reach their ends.
Inputs may be any that keep to these rules, and one draw needn't show every extreme that they name: symmetric: ladder_integrals[a, c] equals ladder_integrals[c, a]. `integral_tiles`: symmetric 0/1 tile list.
All inputs are finite; a program needn't handle non-finite values.
Results may differ from the reference program's by a relative error of at most 0.0046.
Values may be sent and summed in bfloat16 or wider, within the bound.
No kernel may reach another device: no remote copies, remote signals or barrier semaphores. Data moves between devices by JAX's collectives and lax.ppermute only.
A program may use at most 128 MiB of HBM per device.

```python
import math
import jax
import jax.numpy as jnp

TILE = 64
V = 2048
NQ = 1024
JW = 8
OCC = 128
BW = 64
VT = 32


def draw_ladder_integrals(key, part):
    key = jax.random.fold_in(key, 11)
    normal_draw = jax.random.normal(key, (V, V), jnp.float32)
    bound_value = 5.0 / math.sqrt(V)
    values = (normal_draw + normal_draw.T) * 0.5 ** 0.5 / math.sqrt(V)
    return jnp.clip(values, -bound_value, bound_value).astype(jnp.bfloat16)


def draw_integral_tiles(key, part):
    key = jax.random.fold_in(key, 23)
    kept = (jax.random.randint(key, (VT, VT), 0, 4) > 0).astype(jnp.int32)
    row_ids = jnp.arange(VT)[:, None]
    col_ids = jnp.arange(VT)[None, :]
    return jnp.where(row_ids <= col_ids, kept, kept.T)


def place_ends(drawn, own_key, least, high):
    longest = drawn.shape.index(max(drawn.shape))
    spots = []
    for shift in (0, 1):
        where = [jax.random.randint(jax.random.fold_in(own_key, axis), (), 0, length) for axis, length in enumerate(drawn.shape)]
        where[longest] = (where[longest] + shift) % drawn.shape[longest]
        spots.append(tuple(where))
    return drawn.at[spots[0]].set(least).at[spots[1]].set(high)


def steps_of(rng, dims, split, low, largest):
    gain = 1.0
    for position, shards_of in split:
        heights = jax.random.uniform(jax.random.fold_in(jax.random.fold_in(rng, 6), position), (shards_of,), jnp.float32, low / len(split), largest / len(split))
        gain = gain * jnp.repeat(jnp.exp(heights), dims[position] // shards_of).reshape((-1,) + (1,) * (len(dims) - 1 - position))
    return gain


def normal_values(key, shape, deviation, reach, cuts=(), kind=jnp.bfloat16):
    drawn = deviation * jax.random.normal(key, shape, jnp.float32)
    if cuts:
        drawn = drawn * steps_of(key, shape, cuts, -0.22, 0.18)
    return jnp.clip(drawn, -reach, reach).astype(kind)


def setup_inputs(seed: int = 0) -> dict:
    key_list = jax.random.split(jax.random.key(seed), 7)
    amplitudes = normal_values(key_list[0], (V, OCC, JW * BW), 1.0, 6.0, ((0, 8), (1, 32)))
    source_block = normal_values(key_list[1], (V, OCC, JW * BW), 0.5, 4.0, ((0, 8), (1, 32)))
    ladder_integrals = draw_ladder_integrals(jax.random.fold_in(key_list[6], 71), 0)
    cholesky_vectors = normal_values(key_list[3], (V, OCC, NQ), (V * 4) ** -0.5, 0.0625, ((0, 8), (1, 32)))
    integral_tiles = draw_integral_tiles(jax.random.fold_in(key_list[6], 71), 0)
    amplitude_tiles = place_ends((jax.random.randint(key_list[5], (VT, OCC), 0, 4) < 3).astype(jnp.int32), jax.random.fold_in(key_list[5], 1), 0, 1)
    return dict(amplitudes=amplitudes, source_block=source_block, ladder_integrals=ladder_integrals, cholesky_vectors=cholesky_vectors, integral_tiles=integral_tiles, amplitude_tiles=amplitude_tiles)


def expand_tiles(mask, rows, cols):
    return jnp.repeat(jnp.repeat(mask, rows, axis=0), cols, axis=1)


def reference(amplitudes, source_block, ladder_integrals, cholesky_vectors, integral_tiles, amplitude_tiles):
    w_mask = expand_tiles(integral_tiles, TILE, TILE).astype(jnp.bfloat16)
    w_eff = ladder_integrals * w_mask
    a_mask = jnp.repeat(amplitude_tiles, TILE, axis=0).astype(jnp.bfloat16)
    t_eff = amplitudes * a_mask[:, :, None]
    ladder = jnp.dot(w_eff, t_eff.reshape(V, -1), preferred_element_type=jnp.float32)
    chol_flat = cholesky_vectors.reshape(V * OCC, NQ)
    cycle_total = jnp.dot(chol_flat.T, t_eff.reshape(V * OCC, JW * BW), preferred_element_type=jnp.float32)
    cycle_total = cycle_total.astype(jnp.bfloat16)
    cycle = jnp.dot(chol_flat, cycle_total, preferred_element_type=jnp.float32)
    total = source_block.astype(jnp.float32) + ladder.reshape(V, OCC, JW * BW) + cycle.reshape(V, OCC, JW * BW)
    return total.astype(jnp.bfloat16)
```

```python
import jax
import jax.numpy as jnp
from jax import lax
from jax.sharding import Mesh, PartitionSpec as P

TILE = 64
SWAP = [(0, 1), (1, 0)]


def shift(n, d):
    return [(i, (i + d) % n) for i in range(n)]


def pair_sum(partial):
    core = lax.axis_index("c")
    rows = partial.shape[0] // 2
    halves = partial.reshape((2, rows) + partial.shape[1:])
    sent = lax.dynamic_index_in_dim(halves, 1 - core, 0, keepdims=False)
    kept = lax.dynamic_index_in_dim(halves, core, 0, keepdims=False)
    got = lax.ppermute(sent.astype(jnp.bfloat16), "c", SWAP)
    return kept + got.astype(jnp.float32)


def pair_gather(half):
    core = lax.axis_index("c")
    got = lax.ppermute(half, "c", SWAP)
    return jnp.concatenate(
        [jnp.where(core == 0, half, got), jnp.where(core == 0, got, half)], 0
    )


def shards(
    amplitudes, source_block, ladder_integrals, cholesky_vectors, integral_tiles, amplitude_tiles
):
    rows, occ, columns = amplitudes.shape
    total = ladder_integrals.shape[1]
    vectors = cholesky_vectors.shape[2]
    tile_rows = rows // TILE
    ny, nz, nx = lax.axis_size("y"), lax.axis_size("z"), lax.axis_size("x")
    core = lax.axis_index("c")
    x = lax.axis_index("x")
    vir = x * 2 + core
    tile = lax.axis_index("y") * nz + lax.axis_index("z")

    occ_tiles = lax.dynamic_slice(
        amplitude_tiles, (vir * tile_rows, tile * occ), (tile_rows, occ)
    )
    own_mask = jnp.repeat(occ_tiles, TILE, axis=0).astype(jnp.bfloat16)
    t_eff = amplitudes * own_mask[:, :, None]

    t_flat = t_eff.reshape(rows, occ * columns)
    from_left = lax.ppermute(t_flat, "x", shift(nx, 1))
    from_right = lax.ppermute(t_flat, "x", shift(nx, -1))

    partial = lax.dot_general(
        cholesky_vectors.reshape(rows * occ, vectors),
        t_eff.reshape(rows * occ, columns),
        (((0,), (0,)), ((), ())),
        preferred_element_type=jnp.float32,
    )

    row_tiles = lax.dynamic_slice(
        integral_tiles, (vir * tile_rows, 0), (tile_rows, total // TILE)
    )
    w_mask = jnp.repeat(jnp.repeat(row_tiles, TILE, axis=0), TILE, axis=1).astype(jnp.bfloat16)
    w_parts = (ladder_integrals * w_mask).reshape(rows, nx, 2, rows)
    w_keep = lax.dynamic_index_in_dim(w_parts, core, 2, keepdims=False)
    w_send = lax.dynamic_index_in_dim(w_parts, 1 - core, 2, keepdims=False)
    w_other = lax.ppermute(w_send, "c", SWAP)

    s = pair_sum(partial)
    group = ny * nz
    chunk = s.shape[0] // group
    s = lax.all_to_all(
        s.astype(jnp.bfloat16).reshape(group, chunk, columns), ("y", "z"), 0, 0, tiled=True
    )
    s = s.astype(jnp.float32).sum(0)
    sent = s.astype(jnp.bfloat16)
    s = s + sum(
        lax.ppermute(sent, "x", shift(nx, d)).astype(jnp.float32) for d in range(1, nx)
    )
    s = s.astype(jnp.bfloat16)
    s = lax.all_to_all(
        jnp.broadcast_to(s[None], (group, chunk, columns)), ("y", "z"), 0, 0, tiled=True
    )
    cycle_total = pair_gather(s.reshape(group * chunk, columns))
    cycle = jnp.dot(
        cholesky_vectors.reshape(rows * occ, vectors),
        cycle_total,
        preferred_element_type=jnp.float32,
    )

    half = rows // 2
    far_a = lax.ppermute(from_left[:half], "x", shift(nx, 1))
    far_b = lax.ppermute(from_right[half:], "x", shift(nx, -1))

    def of(w, place):
        return lax.dynamic_index_in_dim(w, (place + nx) % nx, 1, keepdims=False)

    def product(w):
        terms = [
            (of(w, x), t_flat),
            (of(w, x - 1), from_left),
            (of(w, x + 1), from_right),
            (of(w, x + 2)[:, :half], far_a),
            (of(w, x + 2)[:, half:], far_b),
        ]
        return sum(jnp.dot(a, b, preferred_element_type=jnp.float32) for a, b in terms)

    got = lax.ppermute(product(w_other).astype(jnp.bfloat16), "c", SWAP)
    ladder = product(w_keep) + got.astype(jnp.float32)
    total = (
        source_block.astype(jnp.float32)
        + ladder.reshape(rows, occ, columns)
        + cycle.reshape(rows, occ, columns)
    )
    return total.astype(jnp.bfloat16)


def solution(mesh):
    split = Mesh(mesh.devices.reshape(4, 8, 4, 2), ("y", "z", "x", "c"))
    rows, cols = ("x", "c"), ("y", "z")
    return jax.shard_map(
        shards,
        mesh=split,
        in_specs=(
            P(rows, cols, None),
            P(rows, cols, None),
            P(rows, None),
            P(rows, cols, None),
            P(),
            P(),
        ),
        out_specs=P(rows, cols, None),
        check_vma=False,
    )
```

```python
import functools

import jax
import jax.numpy as jnp
from jax import lax
from jax.experimental import pallas as pl
from jax.experimental.pallas import tpu as pltpu
from jax.sharding import Mesh, PartitionSpec as P

TILE = 64
SWAP = [(0, 1), (1, 0)]
F32, BF16 = jnp.float32, jnp.bfloat16
VMEM = pl.BlockSpec(memory_space=pltpu.VMEM)
SMEM = pl.BlockSpec(memory_space=pltpu.SMEM)


def shift(n, d):
    return [(i, (i + d) % n) for i in range(n)]


def call(kernel, outs, specs, flops, moved):
    return pl.pallas_call(
        kernel,
        out_shape=outs,
        in_specs=specs,
        out_specs=jax.tree.map(lambda _: VMEM, outs),
        compiler_params=pltpu.CompilerParams(vmem_limit_bytes=40 * 2**20),
        cost_estimate=pl.CostEstimate(flops=flops, bytes_accessed=moved, transcendentals=0),
    )


def column_kernel(mask, half, t, chol, out):
    rows, occ, cols = t.shape
    width = out.shape[0]
    place = lax.broadcasted_iota(jnp.int32, (occ, cols), 0)
    parts = []
    for v in range(rows // TILE):
        keep = jnp.zeros((occ, cols), F32)
        for k in range(occ):
            keep = jnp.where(place == k, mask[v, k].astype(F32), keep)
        parts.append(t[v * TILE:(v + 1) * TILE] * keep.astype(BF16)[None])
    masked = jnp.concatenate(parts, 0).reshape(rows * occ, cols)
    start = pl.multiple_of(half[0] * width, width)
    left = chol[:, :, pl.ds(start, width)].reshape(rows * occ, width)
    out[...] = lax.dot_general(
        left, masked, (((0,), (0,)), ((), ())), preferred_element_type=F32
    ).astype(out.dtype)


def ladder_kernel(n, mask, w_keep, w_send, *refs):
    blocks, (kept, sent) = refs[:n], refs[n:]
    rows, cols = kept.shape[0], blocks[0].shape[2]
    occ = blocks[0].shape[1]
    for k in range(occ):
        parts = []
        for b, block in enumerate(blocks):
            for v in range(block.shape[0] // TILE):
                part = block[v * TILE:(v + 1) * TILE, k, :]
                parts.append(part * mask[b, v, k].astype(F32).astype(BF16))
        right = jnp.concatenate(parts, 0)
        at = slice(k * cols, (k + 1) * cols)
        kept[:, at] = jnp.dot(w_keep[...], right, preferred_element_type=F32).astype(kept.dtype)
        sent[:, at] = jnp.dot(w_send[...], right, preferred_element_type=F32).astype(sent.dtype)


def base_kernel(source, near, far, got_near, got_far, out):
    occ, cols = source.shape[1:]
    for k in range(occ):
        at = slice(k * cols, (k + 1) * cols)
        out[:, k, :] = (
            source[:, k, :].astype(F32)
            + near[:, at]
            + far[:, at]
            + got_near[:, at].astype(F32)
            + got_far[:, at].astype(F32)
        )


def first_kernel(half, chol, ct, out):
    rows, occ, _ = chol.shape
    width = ct.shape[0]
    start = pl.multiple_of(half[0] * width, width)
    left = chol[:, :, pl.ds(start, width)].reshape(rows * occ, width)
    out[...] = jnp.dot(left, ct[...], preferred_element_type=F32)


def last_kernel(half, chol, ct, first, base, out):
    rows, occ, _ = chol.shape
    width = ct.shape[0]
    start = pl.multiple_of(half[0] * width, width)
    left = chol[:, :, pl.ds(start, width)].reshape(rows * occ, width)
    total = first[...] + jnp.dot(left, ct[...], preferred_element_type=F32)
    out[...] = (base[...].reshape(total.shape) + total).astype(BF16).reshape(out.shape)


def shards(
    amplitudes, source_block, ladder_integrals, cholesky_vectors, integral_tiles, amplitude_tiles
):
    rows, occ, columns = amplitudes.shape
    total = ladder_integrals.shape[1]
    vectors = cholesky_vectors.shape[2]
    wide = vectors // 2
    tiles = rows // TILE
    ny, nz, nx = lax.axis_size("y"), lax.axis_size("z"), lax.axis_size("x")
    core, x = lax.axis_index("c"), lax.axis_index("x")
    tile = lax.axis_index("y") * nz + lax.axis_index("z")
    shape = jax.ShapeDtypeStruct

    from_left = lax.ppermute(amplitudes, "x", shift(nx, 1))
    from_right = lax.ppermute(amplitudes, "x", shift(nx, -1))

    masks = lax.dynamic_slice(
        amplitude_tiles.reshape(nx, 2, tiles, -1), (0, core, 0, tile * occ), (nx, 1, tiles, occ)
    )[:, 0]

    def mask_of(place):
        return lax.dynamic_index_in_dim(masks, (place + nx) % nx, 0, keepdims=False)

    mine, other = core[None], 1 - core[None]
    column_flops = 2 * wide * rows * occ * columns
    sent = call(
        column_kernel, shape((wide, columns), BF16), [SMEM, SMEM, VMEM, VMEM], column_flops, 3 << 20
    )(mask_of(x), other, amplitudes, cholesky_vectors)
    got = lax.ppermute(sent, "c", SWAP)
    kept = call(
        column_kernel, shape((wide, columns), F32), [SMEM, SMEM, VMEM, VMEM], column_flops, 3 << 20
    )(mask_of(x), mine, amplitudes, cholesky_vectors)

    group = ny * nx
    chunk = wide // group
    s = (kept + got.astype(F32)).astype(BF16)
    s = lax.all_to_all(s.reshape(group, chunk, columns), ("y", "x"), 0, 0, tiled=True)
    s = s.astype(F32).sum(0).astype(BF16)
    s = lax.all_to_all(
        jnp.broadcast_to(s[None], (nz, chunk, columns)), "z", 0, 0, tiled=True
    )
    s = s.astype(F32).sum(0).astype(BF16)
    s = lax.all_to_all(
        jnp.broadcast_to(s[None], (group, chunk, columns)), ("y", "x"), 0, 0, tiled=True
    )
    ct_mine = s.reshape(wide, columns)
    ct_other = lax.ppermute(ct_mine, "c", SWAP)

    row_tiles = lax.dynamic_slice(
        integral_tiles, ((x * 2 + core) * tiles, 0), (tiles, total // TILE)
    )
    w_mask = jnp.repeat(jnp.repeat(row_tiles, TILE, axis=0), TILE, axis=1).astype(BF16)
    w_parts = (ladder_integrals * w_mask).reshape(rows, nx, 2, rows)
    w_mine = lax.dynamic_index_in_dim(w_parts, core, 2, keepdims=False)
    w_swap = lax.dynamic_index_in_dim(w_parts, 1 - core, 2, keepdims=False)
    w_other = lax.ppermute(w_swap, "c", SWAP)

    def columns_of(w, places):
        return jnp.concatenate(
            [lax.dynamic_index_in_dim(w, (p + nx) % nx, 1, keepdims=False) for p in places], 1
        )

    def products(blocks, places, mask):
        n = len(blocks)
        size = rows * occ * columns
        flops = 4 * size * rows * len(places)
        return call(
            functools.partial(ladder_kernel, n),
            (shape((rows, occ * columns), F32), shape((rows, occ * columns), BF16)),
            [SMEM] + [VMEM] * (2 + n),
            flops,
            len(places) * 4 << 20,
        )(mask, columns_of(w_mine, places), columns_of(w_other, places), *blocks)

    half = rows // 2
    far_a = lax.ppermute(from_left[:half], "x", shift(nx, 1))
    far_b = lax.ppermute(from_right[half:], "x", shift(nx, -1))
    near_places = (x, x - 1, x + 1)
    near, near_sent = products(
        (amplitudes, from_left, from_right),
        near_places,
        jnp.stack([mask_of(p) for p in near_places]),
    )
    got_near = lax.ppermute(near_sent, "c", SWAP)
    far, far_sent = products(
        (far_a, far_b), (x + 2,), mask_of(x + 2).reshape(2, tiles // 2, occ)
    )
    got_far = lax.ppermute(far_sent, "c", SWAP)
    base = call(base_kernel, shape((rows, occ, columns), F32), [VMEM] * 5, 0, 8 << 20)(
        source_block, near, far, got_near, got_far
    )

    first = call(
        first_kernel, shape((rows * occ, columns), F32), [SMEM, VMEM, VMEM], column_flops, 4 << 20
    )(mine, cholesky_vectors, ct_mine)
    return call(
        last_kernel,
        shape((rows, occ, columns), BF16),
        [SMEM, VMEM, VMEM, VMEM, VMEM],
        column_flops,
        6 << 20,
    )(other, cholesky_vectors, ct_other, first, base)


def solution(mesh):
    split = Mesh(mesh.devices.reshape(4, 8, 4, 2), ("y", "z", "x", "c"))
    rows, cols = ("x", "c"), ("y", "z")
    return jax.shard_map(
        shards,
        mesh=split,
        in_specs=(
            P(rows, cols, None),
            P(rows, cols, None),
            P(rows, None),
            P(rows, cols, None),
            P(),
            P(),
        ),
        out_specs=P(rows, cols, None),
        check_vma=False,
    )
```

```python
import functools

import jax
import jax.numpy as jnp
from jax import lax
from jax.experimental import pallas as pl
from jax.experimental.pallas import tpu as pltpu
from jax.sharding import Mesh, PartitionSpec as P

TILE = 64
SWAP = [(0, 1), (1, 0)]
F32, BF16 = jnp.float32, jnp.bfloat16
VMEM = pl.BlockSpec(memory_space=pltpu.VMEM)
SMEM = pl.BlockSpec(memory_space=pltpu.SMEM)
ANY = pl.BlockSpec(memory_space=pl.ANY)
shape = jax.ShapeDtypeStruct


def shift(n, d):
    return [(i, (i + d) % n) for i in range(n)]


def call(kernel, outs, specs, micros, scratch=(), out_space=VMEM):
    return pl.pallas_call(
        kernel,
        out_shape=outs,
        in_specs=specs,
        out_specs=jax.tree.map(lambda _: out_space, outs),
        scratch_shapes=scratch,
        compiler_params=pltpu.CompilerParams(vmem_limit_bytes=24 * 2**20),
        cost_estimate=pl.CostEstimate(
            flops=0, bytes_accessed=int(micros * 3.4e6), transcendentals=0
        ),
    )


def dot(a, b, over=1):
    return lax.dot_general(a, b, (((over,), (0,)), ((), ())), preferred_element_type=F32)


def column_kernel(place, half, mask, t, chol, out, t_buf, chol_buf, sems):
    rows, occ, cols = t.shape
    width = out.shape[0]
    steps = rows // TILE
    start = pl.multiple_of(half[0] * width, width)
    copies = []
    for v in range(steps):
        at = pl.ds(v * TILE, TILE)
        copies.append((
            pltpu.make_async_copy(t.at[at], t_buf.at[v], sems.at[0, v]),
            pltpu.make_async_copy(
                chol.at[at, :, pl.ds(start, width)], chol_buf.at[v], sems.at[1, v]
            ),
        ))
    for pair in copies:
        for copy in pair:
            copy.start()
    k_id = lax.broadcasted_iota(jnp.int32, (occ, cols), 0)
    total = None
    for v in range(steps):
        keep = jnp.zeros((occ, cols), F32)
        for k in range(occ):
            kept = mask[place[0] * steps + v, place[1] * occ + k]
            keep = jnp.where(k_id == k, kept.astype(F32), keep)
        for copy in copies[v]:
            copy.wait()
        masked = (t_buf[v] * keep.astype(BF16)[None]).reshape(TILE * occ, cols)
        term = dot(chol_buf[v].reshape(TILE * occ, width), masked, 0)
        total = term if total is None else total + term
    out[...] = total.astype(out.dtype)


def w_kernel(place, tiles, w, after, mine, other):
    rows = w.shape[0]
    steps = rows // TILE
    ring = mine.shape[1] // rows
    lane = lax.broadcasted_iota(jnp.int32, (TILE, 2 * TILE), 1)
    for d in range(ring):
        for out, core in ((mine, place[3]), (other, 1 - place[3])):
            block = ((place[2] + d) % ring) * 2 + core
            for j in range(rows // (2 * TILE)):
                at = pl.ds(pl.multiple_of(block * rows + j * 2 * TILE, 2 * TILE), 2 * TILE)
                col = block * steps + 2 * j
                for v in range(steps):
                    row = place[0] * steps + v
                    keep = jnp.where(
                        lane < TILE, tiles[row, col].astype(F32), tiles[row, col + 1].astype(F32)
                    )
                    here = slice(v * TILE, (v + 1) * TILE)
                    to = slice(d * rows + j * 2 * TILE, d * rows + (j + 1) * 2 * TILE)
                    out[here, to] = w[here, at] * keep.astype(BF16)


def split_kernel(left, right, after, low, high, sems):
    half = low.shape[0]
    first = pltpu.make_async_copy(left.at[pl.ds(0, half)], low, sems.at[0])
    second = pltpu.make_async_copy(right.at[pl.ds(half, half)], high, sems.at[1])
    first.start()
    second.start()
    first.wait()
    second.wait()


def order(occ):
    n = TILE * occ
    row = lax.broadcasted_iota(jnp.int32, (n, n), 0)
    col = lax.broadcasted_iota(jnp.int32, (n, n), 1)
    return jnp.where(col == (row % TILE) * occ + row // TILE, 1.0, 0.0)


def ladder_kernel(ring, n, last, place, mask, w_mine, w_other, *refs):
    blocks, (kept, sent) = refs[:n], refs[-2:]
    rows = kept.shape[0]
    occ, cols = blocks[0].shape[1:]
    steps = rows // TILE
    perm = order(occ)
    k_id = lax.broadcasted_iota(jnp.int32, perm.shape, 0) // TILE
    right = [[] for _ in range(occ)]
    for b, v0, d in ring:
        block = blocks[b]
        chip = (place[2] + d) % 4
        for v in range(block.shape[0] // TILE):
            scale = jnp.zeros(perm.shape, F32)
            for k in range(occ):
                kept_one = mask[(chip * 2 + place[3]) * steps + v0 + v, place[1] * occ + k]
                scale = jnp.where(k_id == k, kept_one.astype(F32), scale)
            laid = dot(
                (perm * scale).astype(BF16),
                block[v * TILE:(v + 1) * TILE].reshape(TILE * occ, cols),
            ).astype(BF16)
            for k in range(occ):
                right[k].append(laid[k * TILE:(k + 1) * TILE])
    ds = [d for i, (_, _, d) in enumerate(ring) if i == 0 or ring[i - 1][2] != d]
    for k in range(occ):
        at = slice(k * cols, (k + 1) * cols)
        for w, out in ((w_mine, kept), (w_other, sent)):
            total = refs[n + (out is sent)][:, at] if last else None
            for i, d in enumerate(ds):
                part = jnp.concatenate(right[k][i * steps:(i + 1) * steps], 0)
                term = dot(w[:, d * rows:(d + 1) * rows], part)
                total = term if total is None else total + term
            out[:, at] = total.astype(out.dtype)


def base_kernel(source, kept, got, out):
    occ, cols = source.shape[1:]
    rows = source.shape[0]
    back = order(occ).astype(BF16)
    for v in range(rows // TILE):
        here = slice(v * TILE, (v + 1) * TILE)
        whole = jnp.concatenate(
            [
                kept[here, k * cols:(k + 1) * cols]
                + got[here, k * cols:(k + 1) * cols].astype(F32)
                for k in range(occ)
            ],
            0,
        )
        high = whole.astype(BF16)
        low = (whole - high.astype(F32)).astype(BF16)
        out[v * TILE * occ:(v + 1) * TILE * occ] = (
            source[here].reshape(TILE * occ, cols).astype(F32)
            + dot(back, high, 0)
            + dot(back, low, 0)
        )


def first_kernel(half, chol, ct, out):
    rows, occ, _ = chol.shape
    width = ct.shape[0]
    start = pl.multiple_of(half[0] * width, width)
    out[...] = dot(chol[:, :, pl.ds(start, width)].reshape(rows * occ, width), ct[...])


def last_kernel(half, chol, ct, first, base, out):
    rows, occ, _ = chol.shape
    width = ct.shape[0]
    start = pl.multiple_of(half[0] * width, width)
    total = dot(chol[:, :, pl.ds(start, width)].reshape(rows * occ, width), ct[...])
    out[...] = (total + first[...] + base[...]).astype(BF16).reshape(out.shape)


def shards(
    amplitudes, source_block, ladder_integrals, cholesky_vectors, integral_tiles, amplitude_tiles
):
    rows, occ, columns = amplitudes.shape
    vectors = cholesky_vectors.shape[2]
    wide = vectors // 2
    steps = rows // TILE
    ny, nz, nx = lax.axis_size("y"), lax.axis_size("z"), lax.axis_size("x")
    core, x = lax.axis_index("c"), lax.axis_index("x")
    tile = lax.axis_index("y") * nz + lax.axis_index("z")
    place = jnp.stack([x * 2 + core, tile, x, core])
    mine, other = core[None], 1 - core[None]

    from_left = lax.ppermute(amplitudes, "x", shift(nx, 1))
    from_right = lax.ppermute(amplitudes, "x", shift(nx, -1))

    def column(half, kind):
        return call(
            column_kernel,
            shape((wide, columns), kind),
            [SMEM, SMEM, SMEM, ANY, ANY],
            1.5,
            [
                pltpu.VMEM((steps, TILE, occ, columns), BF16),
                pltpu.VMEM((steps, TILE, occ, wide), BF16),
                pltpu.SemaphoreType.DMA((2, steps)),
            ],
        )(place, half, amplitude_tiles, amplitudes, cholesky_vectors)

    got = lax.ppermute(column(other, BF16), "c", SWAP)
    kept = column(mine, F32)

    group = ny * nx
    chunk = wide // group
    s1 = (kept + got.astype(F32)).astype(BF16)
    s = lax.all_to_all(s1.reshape(group, chunk, columns), ("y", "x"), 0, 0, tiled=True)
    s2 = s.astype(F32).sum(0).astype(BF16)
    s = lax.all_to_all(
        jnp.broadcast_to(s2[None], (nz, chunk, columns)), "z", 0, 0, tiled=True
    )
    s3 = s.astype(F32).sum(0).astype(BF16)
    s = lax.all_to_all(
        jnp.broadcast_to(s3[None], (group, chunk, columns)), ("y", "x"), 0, 0, tiled=True
    )
    ct_mine = s.reshape(wide, columns)
    ct_other = lax.ppermute(ct_mine, "c", SWAP)

    w_mine, w_swap = call(
        w_kernel, (shape((rows, nx * rows), BF16),) * 2, [SMEM, SMEM, VMEM, ANY], 1.0
    )(place, integral_tiles, ladder_integrals, s1)
    w_other = lax.ppermute(w_swap, "c", SWAP)

    half = rows // 2
    low, high = call(
        split_kernel,
        (shape((half, occ, columns), BF16),) * 2,
        [ANY, ANY, ANY],
        0.5,
        [pltpu.SemaphoreType.DMA((2,))],
        ANY,
    )(from_left, from_right, s2)
    far_low = lax.ppermute(low, "x", shift(nx, 1))
    far_high = lax.ppermute(high, "x", shift(nx, -1))

    near_kept, near_sent = call(
        functools.partial(ladder_kernel, ((0, 0, 0), (1, 0, -1 % nx), (2, 0, 1)), 3, False),
        (shape((rows, occ * columns), F32),) * 2,
        [SMEM, SMEM] + [VMEM] * 5 + [ANY],
        3.0,
    )(place, amplitude_tiles, w_mine, w_other, amplitudes, from_left, from_right, s3)
    all_kept, all_sent = call(
        functools.partial(ladder_kernel, ((0, 0, 2), (1, steps // 2, 2)), 2, True),
        (shape((rows, occ * columns), F32), shape((rows, occ * columns), BF16)),
        [SMEM, SMEM] + [VMEM] * 6,
        1.2,
    )(place, amplitude_tiles, w_mine, w_other, far_low, far_high, near_kept, near_sent)
    all_got = lax.ppermute(all_sent, "c", SWAP)
    base = call(base_kernel, shape((rows * occ, columns), F32), [VMEM] * 3, 1.2)(
        source_block, all_kept, all_got
    )

    first = call(
        first_kernel, shape((rows * occ, columns), F32), [SMEM, VMEM, VMEM], 0.7
    )(mine, cholesky_vectors, ct_mine)
    return call(
        last_kernel,
        shape((rows, occ, columns), BF16),
        [SMEM, VMEM, VMEM, VMEM, VMEM],
        1.5,
    )(other, cholesky_vectors, ct_other, first, base)


def solution(mesh):
    split = Mesh(mesh.devices.reshape(4, 8, 4, 2), ("y", "z", "x", "c"))
    rows, cols = ("x", "c"), ("y", "z")
    return jax.shard_map(
        shards,
        mesh=split,
        in_specs=(
            P(rows, cols, None),
            P(rows, cols, None),
            P(rows, None),
            P(rows, cols, None),
            P(),
            P(),
        ),
        out_specs=P(rows, cols, None),
        check_vma=False,
    )
```

```python
import functools

import jax
import jax.numpy as jnp
from jax import lax
from jax.experimental import pallas as pl
from jax.experimental.pallas import tpu as pltpu
from jax.sharding import Mesh, PartitionSpec as P

TILE = 64
FULL = 58
SWAP = [(0, 1), (1, 0)]
F32, BF16 = jnp.float32, jnp.bfloat16
VMEM = pl.BlockSpec(memory_space=pltpu.VMEM)
SMEM = pl.BlockSpec(memory_space=pltpu.SMEM)
ANY = pl.BlockSpec(memory_space=pl.ANY)
shape = jax.ShapeDtypeStruct


def shift(n, d):
    return [(i, (i + d) % n) for i in range(n)]


def call(kernel, outs, specs, micros, limit, scratch=(), spaces=None, grid=()):
    return pl.pallas_call(
        kernel,
        out_shape=outs,
        grid=grid,
        in_specs=specs,
        out_specs=spaces or jax.tree.map(lambda _: VMEM, outs),
        scratch_shapes=scratch,
        compiler_params=pltpu.CompilerParams(vmem_limit_bytes=limit * 2**20),
        cost_estimate=pl.CostEstimate(
            flops=0, bytes_accessed=int(micros * 3.4e6), transcendentals=0
        ),
    )


def dot(a, b, over=1):
    return lax.dot_general(a, b, (((over,), (0,)), ((), ())), preferred_element_type=F32)


def column_kernel(vir, tile, half, tiles, t, chol, *refs):
    out, pieces = refs[0], refs[1:-6]
    t_buf, chol_buf, mask, sems, piece_sems, mask_sem = refs[-6:]
    rows, occ, cols = t.shape
    width = out.shape[0]
    steps = rows // TILE
    start = pl.multiple_of(half[0] * width, width)
    mask_copy = pltpu.make_async_copy(tiles, mask, mask_sem)
    mask_copy.start()
    copies = []
    for v in range(steps):
        at = pl.ds(v * TILE, TILE)
        copies.append((
            pltpu.make_async_copy(t.at[at], t_buf.at[v], sems.at[0, v]),
            pltpu.make_async_copy(
                chol.at[at, :, pl.ds(start, width)], chol_buf.at[v], sems.at[1, v]
            ),
        ))
    for pair in copies:
        for copy in pair:
            copy.start()
    k_id = lax.broadcasted_iota(jnp.int32, (occ, cols), 0)
    total = None
    outgoing = []
    mask_copy.wait()
    for v in range(steps):
        keep = jnp.zeros((occ, cols), F32)
        for k in range(occ):
            kept = mask[vir[0] * steps + v, tile[0] * occ + k]
            keep = jnp.where(k_id == k, kept.astype(F32), keep)
        for copy in copies[v]:
            copy.wait()
        for piece in pieces[v * 2 // steps:][:1]:
            here = pl.ds((v % (steps // 2)) * TILE, TILE)
            outgoing.append(pltpu.make_async_copy(t_buf.at[v], piece.at[here], piece_sems.at[v]))
            outgoing[-1].start()
        masked = (t_buf[v] * keep.astype(BF16)[None]).reshape(TILE * occ, cols)
        term = dot(chol_buf[v].reshape(TILE * occ, width), masked, 0)
        total = term if total is None else total + term
    out[...] = total.astype(out.dtype)
    for copy in outgoing:
        copy.wait()


def add_kernel(kept, got, out):
    out[...] = (kept[...] + got[...].astype(F32)).astype(BF16)


def w_kernel(places, vir, x, core, tiles, w, after, mine, other):
    rows = w.shape[0]
    steps = rows // TILE
    ring = len(places)
    lane = lax.broadcasted_iota(jnp.int32, (TILE, 2 * TILE), 1)
    for i, d in enumerate(places):
        for out, which in ((mine, core[0]), (other, 1 - core[0])):
            block = ((x[0] + d) % ring) * 2 + which
            for j in range(rows // (2 * TILE)):
                at = pl.ds(pl.multiple_of(block * rows + j * 2 * TILE, 2 * TILE), 2 * TILE)
                col = block * steps + 2 * j
                for v in range(steps):
                    row = vir[0] * steps + v
                    keep = jnp.where(
                        lane < TILE, tiles[row, col].astype(F32), tiles[row, col + 1].astype(F32)
                    )
                    here = slice(v * TILE, (v + 1) * TILE)
                    to = slice(i * rows + j * 2 * TILE, i * rows + (j + 1) * 2 * TILE)
                    out[here, to] = w[here, at] * keep.astype(BF16)


def pieces_kernel(t, left, right, after, *refs):
    outs, token, held, sems = refs[:4], refs[4], refs[5], refs[6]
    token[...] = jnp.zeros_like(token)
    half = left.shape[0]
    sources = (t.at[pl.ds(0, half)], t.at[pl.ds(half, half)], left, right)
    inward = [
        pltpu.make_async_copy(source, held.at[i], sems.at[0, i])
        for i, source in enumerate(sources)
    ]
    outward = [
        pltpu.make_async_copy(held.at[i], out, sems.at[1, i]) for i, out in enumerate(outs)
    ]
    for copy in inward:
        copy.start()
    for copy, then in zip(inward, outward):
        copy.wait()
        then.start()
    for copy in outward:
        copy.wait()


def pass_kernel(value, after, out):
    out[...] = value[...]


def sum_kernel(parts, *refs):
    out = refs[-1]
    total = parts[0].astype(F32)
    for i in range(1, parts.shape[0]):
        total = total + parts[i].astype(F32)
    total = total.astype(BF16)
    for i in range(out.shape[0]):
        out[i] = total


def permutation(n, occ):
    row = lax.broadcasted_iota(jnp.int32, (n, n), 0)
    col = lax.broadcasted_iota(jnp.int32, (n, n), 1)
    per = n // occ
    return jnp.where(col == (row % per) * occ + row // per, 1.0, 0.0), row // per


def lay_block(block, mask, row, col, right, start):
    rows, occ, cols = block.shape
    perm, k_id = permutation(TILE * occ, occ)
    for v in range(rows // TILE):
        scale = jnp.zeros(perm.shape, F32)
        for k in range(occ):
            scale = jnp.where(k_id == k, mask[row + v, col + k].astype(F32), scale)
        tile = block[v * TILE:(v + 1) * TILE].reshape(TILE * occ, cols)
        laid = dot((perm * scale).astype(BF16), tile).astype(BF16)
        at = slice(start + v * TILE, start + (v + 1) * TILE)
        for k in range(occ):
            right[k, at] = laid[k * TILE:(k + 1) * TILE]


def lay_kernel(ring, x, tile, core, mask, *refs):
    n = len(ring)
    blocks, (out, token), (held, right, in_sems, out_sems) = refs[:n], refs[n:n + 2], refs[n + 2:]
    token[...] = jnp.zeros_like(token)
    occ = blocks[0].shape[1]
    spots = []
    start = 0
    for block in blocks:
        spots.append(pl.ds(start, block.shape[0]))
        start += block.shape[0]
    inward = [
        pltpu.make_async_copy(block, held.at[spot], in_sems.at[i])
        for i, (block, spot) in enumerate(zip(blocks, spots))
    ]
    outward = [
        pltpu.make_async_copy(right.at[:, spot], out.at[:, spot], out_sems.at[i])
        for i, spot in enumerate(spots)
    ]
    for copy in inward:
        copy.start()
    for (v0, d, chips, steps), spot, copy, then in zip(ring, spots, inward, outward):
        copy.wait()
        row = ((x[0] + d) % chips * 2 + core[0]) * steps + v0
        lay_block(held.at[spot], mask, row, tile[0] * occ, right, spot.start)
        then.start()
    for copy in outward:
        copy.wait()


def ladder_kernel(ring, x, tile, core, mask, w_mine, w_other, laid, source, after, *refs):
    n = len(ring)
    blocks, (base, low_sent, high_sent, token) = refs[:n], refs[n:n + 4]
    held, right, w_held, source_held, base_held, sent_held, in_sems, out_sems = refs[n + 4:]
    token[...] = jnp.zeros_like(token)
    rows, occ, cols = source.shape
    steps = rows // TILE
    group = TILE * occ
    near = laid.shape[1]
    spots = []
    start = 0
    for block in blocks:
        spots.append(pl.ds(start, block.shape[0]))
        start += block.shape[0]
    copies = [
        pltpu.make_async_copy(block, held.at[spot], in_sems.at[i])
        for i, (block, spot) in enumerate(zip(blocks, spots))
    ]
    copies += [
        pltpu.make_async_copy(w_other, w_held.at[pl.ds(0, rows)], in_sems.at[n]),
        pltpu.make_async_copy(w_mine, w_held.at[pl.ds(rows, rows)], in_sems.at[n + 1]),
        pltpu.make_async_copy(laid, right.at[:, pl.ds(0, near)], in_sems.at[n + 2]),
        pltpu.make_async_copy(source, source_held, in_sems.at[n + 3]),
    ]
    for copy in copies:
        copy.start()
    for (v0, d, chips, _), spot, copy in zip(ring, spots, copies):
        copy.wait()
        row = ((x[0] + d) % chips * 2 + core[0]) * steps + v0
        lay_block(held.at[spot], mask, row, tile[0] * occ, right, near + spot.start)
    for copy in copies[n:]:
        copy.wait()
    w = w_held[...]
    sums = [dot(w, right[k]).astype(BF16) for k in range(occ)]
    back = permutation(group, occ)[0].astype(BF16)
    outward = []
    for v in range(2 * steps):
        here = slice(v * TILE, (v + 1) * TILE)
        own = dot(back, jnp.concatenate([part[here] for part in sums], 0), 0)
        if v < steps:
            sent_held[v] = own.astype(BF16)
            from_, to = sent_held.at[v], (low_sent, high_sent)[v * 2 // steps]
            at = pl.ds((v % (steps // 2)) * group, group)
        else:
            mine = v - steps
            block = source_held[mine * TILE:(mine + 1) * TILE].reshape(group, cols)
            base_held[mine] = own + block.astype(F32)
            from_, to, at = base_held.at[mine], base, pl.ds(mine * group, group)
        outward.append(pltpu.make_async_copy(from_, to.at[at], out_sems.at[v]))
        outward[-1].start()
    for copy in outward:
        copy.wait()


def first_kernel(half, chol, ct, base, got_low, got_high, out, base_held, got_held, sems):
    rows, occ, _ = chol.shape
    width = ct.shape[0]
    copies = [
        pltpu.make_async_copy(base, base_held, sems.at[0]),
        pltpu.make_async_copy(got_low, got_held.at[0], sems.at[1]),
        pltpu.make_async_copy(got_high, got_held.at[1], sems.at[2]),
    ]
    for copy in copies:
        copy.start()
    start = pl.multiple_of(half[0] * width, width)
    total = dot(chol[:, :, pl.ds(start, width)].reshape(rows * occ, width), ct[...])
    for copy in copies:
        copy.wait()
    size = got_low.shape[0]
    for i in range(2):
        at = slice(i * size, (i + 1) * size)
        out[at] = total[at] + base_held[at] + got_held[i].astype(F32)


def last_kernel(half, chol, ct, first, out):
    rows, occ, _ = chol.shape
    width = ct.shape[0]
    start = pl.multiple_of(half[0] * width, width)
    total = dot(chol[:, :, pl.ds(start, width)].reshape(rows * occ, width), ct[...])
    out[...] = (total + first[...]).astype(BF16).reshape(out.shape)


def shards(
    amplitudes, source_block, ladder_integrals, cholesky_vectors, integral_tiles, amplitude_tiles
):
    rows, occ, columns = amplitudes.shape
    vectors = cholesky_vectors.shape[2]
    wide = vectors // 2
    steps = rows // TILE
    ny, nz, nx = lax.axis_size("y"), lax.axis_size("z"), lax.axis_size("x")
    core, x = lax.axis_index("c"), lax.axis_index("x")
    tile = lax.axis_index("y") * nz + lax.axis_index("z")
    vir = (x * 2 + core)[None]
    tile, x, mine, other = tile[None], x[None], core[None], 1 - core[None]

    row_half = rows // 2
    piece = shape((row_half, occ, columns), BF16)
    token = shape((8, 128), F32)

    def column(half, outs, spaces, micros, limit):
        return call(
            column_kernel,
            outs,
            [SMEM] * 3 + [ANY] * 3,
            micros,
            limit,
            [
                pltpu.VMEM((steps, TILE, occ, columns), BF16),
                pltpu.VMEM((steps, TILE, occ, wide), BF16),
                pltpu.SMEM(amplitude_tiles.shape, jnp.int32),
                pltpu.SemaphoreType.DMA((2, steps)),
                pltpu.SemaphoreType.DMA((steps,)),
                pltpu.SemaphoreType.DMA(()),
            ],
            spaces,
        )(vir, tile, half, amplitude_tiles, amplitudes, cholesky_vectors)

    sent, low, high = column(
        other, (shape((wide, columns), BF16), piece, piece), (VMEM, ANY, ANY), 3.0, FULL
    )
    got = lax.ppermute(sent, "c", SWAP)
    left_low = lax.ppermute(low, "x", shift(nx, 1))
    right_high = lax.ppermute(high, "x", shift(nx, -1))
    (kept,) = column(mine, (shape((wide, columns), F32),), (VMEM,), 2.0, 16)

    group = ny * nx
    chunk = wide // group
    added = call(add_kernel, shape((wide, columns), BF16), [VMEM] * 2, 0.7, 8)(kept, got)
    s1 = lax.all_to_all(added.reshape(group, chunk, columns), ("y", "x"), 0, 0, tiled=True)

    places = (0, nx - 1, 1, 2)
    w_mine, w_swap = call(
        functools.partial(w_kernel, places),
        (shape((rows, nx * rows), BF16),) * 2,
        [SMEM] * 4 + [VMEM, ANY],
        1.9,
        FULL,
    )(vir, x, mine, integral_tiles, ladder_integrals, added)
    w_other = lax.ppermute(w_swap, "c", SWAP)

    low, high, go_right, go_left, after_pieces = call(
        pieces_kernel,
        (piece,) * 4 + (token,),
        [ANY] * 4,
        1.5,
        FULL,
        [pltpu.VMEM((4,) + piece.shape, BF16), pltpu.SemaphoreType.DMA((2, 4))],
        (ANY,) * 4 + (VMEM,),
    )(amplitudes, left_low, right_high, w_swap)
    left_high = lax.ppermute(high, "x", shift(nx, 1))
    right_low = lax.ppermute(low, "x", shift(nx, -1))
    far_low = lax.ppermute(go_right, "x", shift(nx, 1))
    far_high = lax.ppermute(go_left, "x", shift(nx, -1))

    def summed(receivers, *parts):
        return call(
            sum_kernel,
            shape((receivers, chunk, columns), BF16),
            [VMEM] * len(parts),
            1.0,
            8,
        )(*parts)

    s2 = lax.all_to_all(summed(nz, s1, after_pieces), "z", 0, 0, tiled=True)
    mid = steps // 2
    near_ring = tuple(
        (v0, d, nx, steps) for v0, d in ((0, 0), (0, nx - 1), (mid, nx - 1), (0, 1), (mid, 1))
    )
    near_blocks = (amplitudes, left_low, left_high, right_low, right_high)
    near = 3 * rows
    laid, after_lay = call(
        functools.partial(lay_kernel, near_ring),
        (shape((occ, near, columns), BF16), token),
        [SMEM] * 4 + [ANY] * len(near_blocks),
        3.0,
        FULL,
        [
            pltpu.VMEM((near, occ, columns), BF16),
            pltpu.VMEM((occ, near, columns), BF16),
            pltpu.SemaphoreType.DMA((len(near_blocks),)),
            pltpu.SemaphoreType.DMA((len(near_blocks),)),
        ],
        (ANY, VMEM),
    )(x, tile, mine, amplitude_tiles, *near_blocks)

    third = summed(group, s2, after_lay)
    s3 = lax.all_to_all(third, ("y", "x"), 0, 0, tiled=True)

    half_out = shape((rows * occ // 2, columns), BF16)
    base, low_sent, high_sent, after_ladder = call(
        functools.partial(ladder_kernel, ((0, 2, nx, steps), (mid, 2, nx, steps))),
        (shape((rows * occ, columns), F32), half_out, half_out, token),
        [SMEM] * 4 + [ANY] * 7,
        5.0,
        56,
        [
            pltpu.VMEM((rows, occ, columns), BF16),
            pltpu.VMEM((occ, nx * rows, columns), BF16),
            pltpu.VMEM((2 * rows, nx * rows), BF16),
            pltpu.VMEM((rows, occ, columns), BF16),
            pltpu.VMEM((steps, TILE * occ, columns), F32),
            pltpu.VMEM((steps, TILE * occ, columns), BF16),
            pltpu.SemaphoreType.DMA((6,)),
            pltpu.SemaphoreType.DMA((2 * steps,)),
        ],
        (ANY, ANY, ANY, VMEM),
    )(
        x, tile, mine, amplitude_tiles, w_mine, w_other, laid, source_block, third, far_low,
        far_high,
    )
    low_got = lax.ppermute(low_sent, "c", SWAP)
    high_got = lax.ppermute(high_sent, "c", SWAP)
    ct_mine = call(pass_kernel, shape((wide, columns), BF16), [VMEM] * 2, 0.4, 8)(
        s3.reshape(wide, columns), after_ladder
    )
    ct_other = lax.ppermute(ct_mine, "c", SWAP)
    first = call(
        first_kernel,
        shape((rows * occ, columns), F32),
        [SMEM] + [VMEM] * 2 + [ANY] * 3,
        1.2,
        16,
        [
            pltpu.VMEM((rows * occ, columns), F32),
            pltpu.VMEM((2,) + half_out.shape, BF16),
            pltpu.SemaphoreType.DMA((3,)),
        ],
    )(mine, cholesky_vectors, ct_mine, base, low_got, high_got)
    return call(
        last_kernel, shape((rows, occ, columns), BF16), [SMEM] + [VMEM] * 3, 1.5, 16
    )(other, cholesky_vectors, ct_other, first)


def solution(mesh):
    split = Mesh(mesh.devices.reshape(4, 8, 4, 2), ("y", "z", "x", "c"))
    rows, cols = ("x", "c"), ("y", "z")
    return jax.shard_map(
        shards,
        mesh=split,
        in_specs=(
            P(rows, cols, None),
            P(rows, cols, None),
            P(rows, None),
            P(rows, cols, None),
            P(),
            P(),
        ),
        out_specs=P(rows, cols, None),
        check_vma=False,
    )
```

```python
import functools

import jax
import jax.numpy as jnp
from jax import lax
from jax.experimental import pallas as pl
from jax.experimental.pallas import tpu as pltpu
from jax.sharding import Mesh, PartitionSpec as P

TILE = 64
FULL = 58
SWAP = [(0, 1), (1, 0)]
F32, BF16 = jnp.float32, jnp.bfloat16
VMEM = pl.BlockSpec(memory_space=pltpu.VMEM)
SMEM = pl.BlockSpec(memory_space=pltpu.SMEM)
ANY = pl.BlockSpec(memory_space=pl.ANY)
shape = jax.ShapeDtypeStruct


def shift(n, d):
    return [(i, (i + d) % n) for i in range(n)]


def call(kernel, outs, specs, micros, limit, scratch=(), spaces=None, grid=()):
    return pl.pallas_call(
        kernel,
        out_shape=outs,
        grid=grid,
        in_specs=specs,
        out_specs=spaces or jax.tree.map(lambda _: VMEM, outs),
        scratch_shapes=scratch,
        compiler_params=pltpu.CompilerParams(vmem_limit_bytes=limit * 2**20),
        cost_estimate=pl.CostEstimate(
            flops=0, bytes_accessed=int(micros * 3.4e6), transcendentals=0
        ),
    )


def dot(a, b, over=1):
    return lax.dot_general(a, b, (((over,), (0,)), ((), ())), preferred_element_type=F32)


def permutation(n, occ):
    row = lax.broadcasted_iota(jnp.int32, (n, n), 0)
    col = lax.broadcasted_iota(jnp.int32, (n, n), 1)
    per = n // occ
    return jnp.where(col == (row % per) * occ + row // per, 1.0, 0.0).astype(BF16)


def column_kernel(vir, tile, half, tiles, t, chol, *refs):
    out, pieces = refs[0], refs[1:-7]
    t_buf, chol_buf, laid, mask, sems, piece_sems, mask_sem = refs[-7:]
    rows, occ, cols = t.shape
    width = out.shape[0]
    steps = rows // TILE
    start = pl.multiple_of(half[0] * width, width)
    mask_copy = pltpu.make_async_copy(tiles, mask, mask_sem)
    mask_copy.start()
    copies = []
    for v in range(steps):
        at = pl.ds(v * TILE, TILE)
        copies.append((
            pltpu.make_async_copy(t.at[at], t_buf.at[v], sems.at[0, v]),
            pltpu.make_async_copy(
                chol.at[at, :, pl.ds(start, width)], chol_buf.at[v], sems.at[1, v]
            ),
        ))
    for pair in copies:
        for copy in pair:
            copy.start()
    k_id = lax.broadcasted_iota(jnp.int32, (occ, cols), 0)
    perm = permutation(TILE * occ, occ)
    total = None
    outgoing = []
    mask_copy.wait()
    for v in range(steps):
        keep = jnp.zeros((occ, cols), F32)
        for k in range(occ):
            kept = mask[vir[0] * steps + v, tile[0] * occ + k]
            keep = jnp.where(k_id == k, kept.astype(F32), keep)
        for copy in copies[v]:
            copy.wait()
        masked = (t_buf[v] * keep.astype(BF16)[None]).reshape(TILE * occ, cols)
        if pieces:
            moved = dot(perm, masked).astype(BF16)
            which, place = divmod(v, steps // 2)
            for k in range(occ):
                laid[which, k, place * TILE:(place + 1) * TILE] = moved[k * TILE:(k + 1) * TILE]
            if place == steps // 2 - 1:
                outgoing.append(
                    pltpu.make_async_copy(laid.at[which], pieces[which], piece_sems.at[which])
                )
                outgoing[-1].start()
        term = dot(chol_buf[v].reshape(TILE * occ, width), masked, 0)
        total = term if total is None else total + term
    out[...] = total.astype(out.dtype)
    for copy in outgoing:
        copy.wait()


def add_kernel(kept, got, out):
    out[...] = (kept[...] + got[...].astype(F32)).astype(BF16)


def w_kernel(places, vir, x, core, tiles, w, after, mine, other):
    rows = w.shape[0]
    steps = rows // TILE
    ring = len(places)
    lane = lax.broadcasted_iota(jnp.int32, (TILE, 2 * TILE), 1)
    for i, d in enumerate(places):
        for out, which in ((mine, core[0]), (other, 1 - core[0])):
            block = ((x[0] + d) % ring) * 2 + which
            for j in range(rows // (2 * TILE)):
                at = pl.ds(pl.multiple_of(block * rows + j * 2 * TILE, 2 * TILE), 2 * TILE)
                col = block * steps + 2 * j
                for v in range(steps):
                    row = vir[0] * steps + v
                    keep = jnp.where(
                        lane < TILE, tiles[row, col].astype(F32), tiles[row, col + 1].astype(F32)
                    )
                    here = slice(v * TILE, (v + 1) * TILE)
                    to = slice(i * rows + j * 2 * TILE, i * rows + (j + 1) * 2 * TILE)
                    out[here, to] = w[here, at] * keep.astype(BF16)


def pieces_kernel(low, high, left, right, after, to_right, to_left, held, sems):
    pairs = (
        (high, to_right.at[0]), (low, to_left.at[0]), (left, to_right.at[1]), (right, to_left.at[1])
    )
    inward = [
        pltpu.make_async_copy(source, held.at[i], sems.at[0, i])
        for i, (source, _) in enumerate(pairs)
    ]
    outward = [
        pltpu.make_async_copy(held.at[i], out, sems.at[1, i]) for i, (_, out) in enumerate(pairs)
    ]
    for copy in inward:
        copy.start()
    for copy, then in zip(inward, outward):
        copy.wait()
        then.start()
    for copy in outward:
        copy.wait()


def sum_kernel(parts, *refs):
    out = refs[-1]
    total = parts[0].astype(F32)
    for i in range(1, parts.shape[0]):
        total = total + parts[i].astype(F32)
    total = total.astype(BF16)
    for i in range(out.shape[0]):
        out[i] = total


def ladder_kernel(
    w_mine, w_other, source, low, high, left_low, right_high, from_left, from_right, after,
    base, low_sent, high_sent, right, w_held, source_held, base_held, sent_held, in_sems, out_sems,
):
    rows, occ, cols = source.shape
    pieces = (
        low, high, left_low, from_left.at[0], from_right.at[0], right_high, from_left.at[1],
        from_right.at[1],
    )
    steps = rows // TILE
    group = TILE * occ
    size = pieces[0].shape[1]
    w_copies = [
        pltpu.make_async_copy(w_other, w_held.at[pl.ds(0, rows)], in_sems.at[len(pieces), 0]),
        pltpu.make_async_copy(w_mine, w_held.at[pl.ds(rows, rows)], in_sems.at[len(pieces), 1]),
    ]
    source_copy = pltpu.make_async_copy(source, source_held, in_sems.at[len(pieces), 2])
    copies = [
        [
            pltpu.make_async_copy(
                piece.at[k], right.at[k, pl.ds(i * size, size)], in_sems.at[i, k]
            )
            for i, piece in enumerate(pieces)
        ]
        for k in range(occ)
    ]
    for copy in w_copies + sum(copies, []) + [source_copy]:
        copy.start()
    back = permutation(group, occ)
    for copy in w_copies:
        copy.wait()
    w = w_held[...]
    sums = []
    for k in range(occ):
        for copy in copies[k]:
            copy.wait()
        sums.append(dot(w, right[k]).astype(BF16))
    source_copy.wait()
    outward = []
    for v in range(2 * steps):
        here = slice(v * TILE, (v + 1) * TILE)
        own = dot(back, jnp.concatenate([part[here] for part in sums], 0), 0)
        if v < steps:
            sent_held[v] = own.astype(BF16)
            from_, to = sent_held.at[v], (low_sent, high_sent)[v * 2 // steps]
            at = pl.ds((v % (steps // 2)) * group, group)
        else:
            mine = v - steps
            block = source_held[mine * TILE:(mine + 1) * TILE].reshape(group, cols)
            base_held[mine] = (own + block.astype(F32)).astype(BF16)
            from_, to, at = base_held.at[mine], base, pl.ds(mine * group, group)
        outward.append(pltpu.make_async_copy(from_, to.at[at], out_sems.at[v]))
        outward[-1].start()
    for copy in outward:
        copy.wait()


def first_kernel(half, chol, ct, base, out):
    rows, occ, _ = chol.shape
    width = ct.shape[0]
    start = pl.multiple_of(half[0] * width, width)
    total = dot(chol[:, :, pl.ds(start, width)].reshape(rows * occ, width), ct[...])
    out[...] = total + base[...].astype(F32)


def last_kernel(half, chol, ct, first, got_low, got_high, out):
    rows, occ, _ = chol.shape
    width = ct.shape[0]
    start = pl.multiple_of(half[0] * width, width)
    total = dot(chol[:, :, pl.ds(start, width)].reshape(rows * occ, width), ct[...])
    size = got_low.shape[0]
    for i, got in enumerate((got_low, got_high)):
        at = slice(i * size, (i + 1) * size)
        part = total[at] + (first[at] + got[...].astype(F32))
        here = slice(i * rows // 2, (i + 1) * rows // 2)
        out[here] = part.astype(BF16).reshape(rows // 2, occ, out.shape[2])


def shards(
    amplitudes, source_block, ladder_integrals, cholesky_vectors, integral_tiles, amplitude_tiles
):
    rows, occ, columns = amplitudes.shape
    vectors = cholesky_vectors.shape[2]
    wide = vectors // 2
    steps = rows // TILE
    ny, nz, nx = lax.axis_size("y"), lax.axis_size("z"), lax.axis_size("x")
    core, x = lax.axis_index("c"), lax.axis_index("x")
    tile = lax.axis_index("y") * nz + lax.axis_index("z")
    vir = (x * 2 + core)[None]
    tile, x, mine, other = tile[None], x[None], core[None], 1 - core[None]

    row_half = rows // 2
    piece = shape((occ, row_half, columns), BF16)

    def column(half, outs, spaces, micros, limit):
        return call(
            column_kernel,
            outs,
            [SMEM] * 3 + [ANY] * 3,
            micros,
            limit,
            [
                pltpu.VMEM((steps, TILE, occ, columns), BF16),
                pltpu.VMEM((steps, TILE, occ, wide), BF16),
                pltpu.VMEM((2,) + piece.shape, BF16),
                pltpu.SMEM(amplitude_tiles.shape, jnp.int32),
                pltpu.SemaphoreType.DMA((2, steps)),
                pltpu.SemaphoreType.DMA((2,)),
                pltpu.SemaphoreType.DMA(()),
            ],
            spaces,
        )(vir, tile, half, amplitude_tiles, amplitudes, cholesky_vectors)

    sent, low, high = column(
        other, (shape((wide, columns), BF16), piece, piece), (VMEM, ANY, ANY), 3.0, FULL
    )
    got = lax.ppermute(sent, "c", SWAP)
    left_low = lax.ppermute(low, "x", shift(nx, 1))
    right_high = lax.ppermute(high, "x", shift(nx, -1))
    (kept,) = column(mine, (shape((wide, columns), F32),), (VMEM,), 2.0, 16)

    group = ny * nx
    chunk = wide // group
    added = call(add_kernel, shape((wide, columns), BF16), [VMEM] * 2, 0.7, 8)(kept, got)
    plane = [[(i + group // 2 + nx // 2) % group for i in range(group)]]
    line = [[(i + nz // 2) % nz for i in range(nz)]]

    def exchange(parts, axes, members):
        return lax.all_to_all(parts, axes, 0, 0, axis_index_groups=members, tiled=True)

    s1 = exchange(added.reshape(group, chunk, columns), ("y", "x"), plane)

    places = (0, nx - 1, 1, 2)
    w_mine, w_swap = call(
        functools.partial(w_kernel, places),
        (shape((rows, nx * rows), BF16),) * 2,
        [SMEM] * 4 + [VMEM, ANY],
        1.9,
        FULL,
    )(vir, x, mine, integral_tiles, ladder_integrals, added)
    w_other = lax.ppermute(w_swap, "c", SWAP)

    pair = shape((2,) + piece.shape, BF16)
    to_right, to_left = call(
        pieces_kernel,
        (pair, pair),
        [ANY] * 5,
        1.5,
        FULL,
        [pltpu.VMEM((4,) + piece.shape, BF16), pltpu.SemaphoreType.DMA((2, 4))],
        (ANY,) * 2,
    )(low, high, left_low, right_high, w_swap)
    from_left = lax.ppermute(to_right, "x", shift(nx, 1))
    from_right = lax.ppermute(to_left, "x", shift(nx, -1))

    def summed(receivers, *parts):
        return call(
            sum_kernel,
            shape((receivers, chunk, columns), BF16),
            [VMEM] * len(parts),
            1.0,
            8,
        )(*parts)

    s2 = exchange(summed(nz, s1), "z", line)
    third = summed(group, s2)
    s3 = exchange(third, ("y", "x"), plane)

    half_out = shape((rows * occ // 2, columns), BF16)
    base, low_sent, high_sent = call(
        ladder_kernel,
        (shape((rows * occ, columns), BF16), half_out, half_out),
        [ANY] * 10,
        5.0,
        FULL,
        [
            pltpu.VMEM((occ, nx * rows, columns), BF16),
            pltpu.VMEM((2 * rows, nx * rows), BF16),
            pltpu.VMEM((rows, occ, columns), BF16),
            pltpu.VMEM((steps, TILE * occ, columns), BF16),
            pltpu.VMEM((steps, TILE * occ, columns), BF16),
            pltpu.SemaphoreType.DMA((9, occ)),
            pltpu.SemaphoreType.DMA((2 * steps,)),
        ],
        (ANY, ANY, ANY),
    )(
        w_mine, w_other, source_block, low, high, left_low, right_high, from_left, from_right, third
    )
    low_got = lax.ppermute(low_sent, "c", SWAP)
    high_got = lax.ppermute(high_sent, "c", SWAP)
    ct_mine = s3.reshape(wide, columns)
    ct_other = lax.ppermute(ct_mine, "c", SWAP)
    first = call(
        first_kernel, shape((rows * occ, columns), F32), [SMEM] + [VMEM] * 3, 0.9, 12
    )(mine, cholesky_vectors, ct_mine, base)
    return call(
        last_kernel, shape((rows, occ, columns), BF16), [SMEM] + [VMEM] * 5, 2.0, 16
    )(other, cholesky_vectors, ct_other, first, low_got, high_got)


def solution(mesh):
    split = Mesh(mesh.devices.reshape(4, 8, 4, 2), ("y", "z", "x", "c"))
    rows, cols = ("x", "c"), ("y", "z")
    return jax.shard_map(
        shards,
        mesh=split,
        in_specs=(
            P(rows, cols, None),
            P(rows, cols, None),
            P(rows, None),
            P(rows, cols, None),
            P(),
            P(),
        ),
        out_specs=P(rows, cols, None),
        check_vma=False,
    )
```

```python
import functools

import jax
import jax.numpy as jnp
from jax import lax
from jax.experimental import pallas as pl
from jax.experimental.pallas import tpu as pltpu
from jax.sharding import Mesh, PartitionSpec as P

TILE = 64
FULL = 58
SWAP = [(0, 1), (1, 0)]
F32, BF16 = jnp.float32, jnp.bfloat16
VMEM = pl.BlockSpec(memory_space=pltpu.VMEM)
SMEM = pl.BlockSpec(memory_space=pltpu.SMEM)
ANY = pl.BlockSpec(memory_space=pl.ANY)
shape = jax.ShapeDtypeStruct


def shift(n, d):
    return [(i, (i + d) % n) for i in range(n)]


def call(kernel, outs, specs, micros, limit, scratch=(), spaces=None, grid=()):
    return pl.pallas_call(
        kernel,
        out_shape=outs,
        grid=grid,
        in_specs=specs,
        out_specs=spaces or jax.tree.map(lambda _: VMEM, outs),
        scratch_shapes=scratch,
        compiler_params=pltpu.CompilerParams(vmem_limit_bytes=limit * 2**20),
        cost_estimate=pl.CostEstimate(
            flops=0, bytes_accessed=int(micros * 3.4e6), transcendentals=0
        ),
    )


def dot(a, b, over=1):
    return lax.dot_general(a, b, (((over,), (0,)), ((), ())), preferred_element_type=F32)


def permutation(n, occ):
    row = lax.broadcasted_iota(jnp.int32, (n, n), 0)
    col = lax.broadcasted_iota(jnp.int32, (n, n), 1)
    per = n // occ
    return jnp.where(col == (row % per) * occ + row // per, 1.0, 0.0).astype(BF16)


def column_kernel(vir, tile, half, tiles, t, chol, out, *refs):
    pieces = refs[:-10]
    t_buf, masked, chol_buf, out_buf, laid, mask, t_sems, sems, piece_sems, mask_sem = refs[-10:]
    rows, occ, cols = t.shape
    parts, width = out_buf.shape[:2]
    steps = rows // TILE
    group = TILE * occ
    start = pl.multiple_of(half[0] * parts * width, parts * width)
    mask_copy = pltpu.make_async_copy(tiles, mask, mask_sem)
    t_copies = [
        pltpu.make_async_copy(t.at[pl.ds(v * TILE, TILE)], t_buf.at[v], t_sems.at[v])
        for v in range(steps)
    ]
    chol_copies = [
        pltpu.make_async_copy(
            chol.at[:, :, pl.ds(start + i * width, width)], chol_buf.at[i], sems.at[0, i]
        )
        for i in range(parts)
    ]
    for copy in [mask_copy] + t_copies + chol_copies:
        copy.start()
    k_id = lax.broadcasted_iota(jnp.int32, (occ, cols), 0)
    perm = permutation(group, occ)
    outgoing = []
    mask_copy.wait()
    for v in range(steps):
        keep = jnp.zeros((occ, cols), F32)
        for k in range(occ):
            kept = mask[vir[0] * steps + v, tile[0] * occ + k]
            keep = jnp.where(k_id == k, kept.astype(F32), keep)
        t_copies[v].wait()
        here = (t_buf[v] * keep.astype(BF16)[None]).reshape(group, cols)
        masked[v * group:(v + 1) * group] = here
        if pieces:
            moved = dot(perm, here).astype(BF16)
            which, place = divmod(v, steps // 2)
            for k in range(occ):
                laid[which, k, place * TILE:(place + 1) * TILE] = moved[k * TILE:(k + 1) * TILE]
            if place == steps // 2 - 1:
                outgoing.append(
                    pltpu.make_async_copy(laid.at[which], pieces[which], piece_sems.at[which])
                )
                outgoing[-1].start()
    for i in range(parts):
        chol_copies[i].wait()
        left = chol_buf[i].reshape(rows * occ, width)
        out_buf[i] = dot(left, masked[...], 0).astype(out_buf.dtype)
        outgoing.append(
            pltpu.make_async_copy(out_buf.at[i], out.at[pl.ds(i * width, width)], sems.at[1, i])
        )
        outgoing[-1].start()
    for copy in outgoing:
        copy.wait()


def add_kernel(kept, got, out):
    out[...] = (kept[...] + got[...].astype(F32)).astype(BF16)


def w_kernel(places, vir, x, core, tiles, w, after, mine, other):
    rows = w.shape[0]
    steps = rows // TILE
    ring = len(places)
    lane = lax.broadcasted_iota(jnp.int32, (TILE, 2 * TILE), 1)
    for i, d in enumerate(places):
        for out, which in ((mine, core[0]), (other, 1 - core[0])):
            block = ((x[0] + d) % ring) * 2 + which
            for j in range(rows // (2 * TILE)):
                at = pl.ds(pl.multiple_of(block * rows + j * 2 * TILE, 2 * TILE), 2 * TILE)
                col = block * steps + 2 * j
                for v in range(steps):
                    row = vir[0] * steps + v
                    keep = jnp.where(
                        lane < TILE, tiles[row, col].astype(F32), tiles[row, col + 1].astype(F32)
                    )
                    here = slice(v * TILE, (v + 1) * TILE)
                    to = slice(i * rows + j * 2 * TILE, i * rows + (j + 1) * 2 * TILE)
                    out[here, to] = w[here, at] * keep.astype(BF16)


def pieces_kernel(low, high, left, right, after, to_right, to_left, held, sems):
    pairs = (
        (high, to_right.at[0]), (low, to_left.at[0]), (left, to_right.at[1]), (right, to_left.at[1])
    )
    inward = [
        pltpu.make_async_copy(source, held.at[i], sems.at[0, i])
        for i, (source, _) in enumerate(pairs)
    ]
    outward = [
        pltpu.make_async_copy(held.at[i], out, sems.at[1, i]) for i, (_, out) in enumerate(pairs)
    ]
    for copy in inward:
        copy.start()
    for copy, then in zip(inward, outward):
        copy.wait()
        then.start()
    for copy in outward:
        copy.wait()


def sum_kernel(parts, *refs):
    out = refs[-1]
    total = parts[0].astype(F32)
    for i in range(1, parts.shape[0]):
        total = total + parts[i].astype(F32)
    total = total.astype(BF16)
    for i in range(out.shape[0]):
        out[i] = total


def ladder_kernel(
    w_mine, w_other, source, low, high, left_low, right_high, from_left, from_right, after,
    base, low_sent, high_sent, right, w_held, source_held, base_held, sent_held, in_sems, out_sems,
):
    rows, occ, cols = source.shape
    pieces = (
        low, high, left_low, from_left.at[0], from_right.at[0], right_high, from_left.at[1],
        from_right.at[1],
    )
    steps = rows // TILE
    group = TILE * occ
    size = pieces[0].shape[1]
    w_copies = [
        pltpu.make_async_copy(w_other, w_held.at[pl.ds(0, rows)], in_sems.at[len(pieces), 0]),
        pltpu.make_async_copy(w_mine, w_held.at[pl.ds(rows, rows)], in_sems.at[len(pieces), 1]),
    ]
    source_copy = pltpu.make_async_copy(source, source_held, in_sems.at[len(pieces), 2])
    copies = [
        [
            pltpu.make_async_copy(
                piece.at[k], right.at[k, pl.ds(i * size, size)], in_sems.at[i, k]
            )
            for i, piece in enumerate(pieces)
        ]
        for k in range(occ)
    ]
    for copy in w_copies + sum(copies, []) + [source_copy]:
        copy.start()
    back = permutation(group, occ)
    for copy in w_copies:
        copy.wait()
    w = w_held[...]
    sums = []
    for k in range(occ):
        for copy in copies[k]:
            copy.wait()
        sums.append(dot(w, right[k]).astype(BF16))
    source_copy.wait()
    outward = []
    for v in range(2 * steps):
        here = slice(v * TILE, (v + 1) * TILE)
        own = dot(back, jnp.concatenate([part[here] for part in sums], 0), 0)
        if v < steps:
            sent_held[v] = own.astype(BF16)
            from_, to = sent_held.at[v], (low_sent, high_sent)[v * 2 // steps]
            at = pl.ds((v % (steps // 2)) * group, group)
        else:
            mine = v - steps
            block = source_held[mine * TILE:(mine + 1) * TILE].reshape(group, cols)
            base_held[mine] = (own + block.astype(F32)).astype(BF16)
            from_, to, at = base_held.at[mine], base, pl.ds(mine * group, group)
        outward.append(pltpu.make_async_copy(from_, to.at[at], out_sems.at[v]))
        outward[-1].start()
    for copy in outward:
        copy.wait()


def first_kernel(half, chol, ct, base, out):
    rows, occ, _ = chol.shape
    width = ct.shape[0]
    start = pl.multiple_of(half[0] * width, width)
    total = dot(chol[:, :, pl.ds(start, width)].reshape(rows * occ, width), ct[...])
    out[...] = total + base[...].astype(F32)


def last_kernel(half, chol, ct, first, got_low, got_high, out, held, sems):
    rows, occ, _ = chol.shape
    width = ct.shape[0]
    steps = held.shape[0]
    each = rows // steps
    group = each * occ
    start = pl.multiple_of(half[0] * width, width)
    copies = []
    for v in range(steps):
        here = slice(v * each, (v + 1) * each)
        total = dot(chol[here, :, pl.ds(start, width)].reshape(group, width), ct[...])
        got = (got_low, got_high)[v * 2 // steps]
        at = (v % (steps // 2)) * group
        part = first[v * group:(v + 1) * group] + got[at:at + group].astype(F32)
        held[v] = (total + part).astype(BF16).reshape(held.shape[1:])
        copies.append(
            pltpu.make_async_copy(held.at[v], out.at[pl.ds(v * each, each)], sems.at[v])
        )
        copies[-1].start()
    for copy in copies:
        copy.wait()


def shards(
    amplitudes, source_block, ladder_integrals, cholesky_vectors, integral_tiles, amplitude_tiles
):
    rows, occ, columns = amplitudes.shape
    vectors = cholesky_vectors.shape[2]
    wide = vectors // 2
    steps = rows // TILE
    ny, nz, nx = lax.axis_size("y"), lax.axis_size("z"), lax.axis_size("x")
    core, x = lax.axis_index("c"), lax.axis_index("x")
    tile = lax.axis_index("y") * nz + lax.axis_index("z")
    vir = (x * 2 + core)[None]
    tile, x, mine, other = tile[None], x[None], core[None], 1 - core[None]

    row_half = rows // 2
    piece = shape((occ, row_half, columns), BF16)

    def column(half, outs, spaces, micros, limit):
        return call(
            column_kernel,
            outs,
            [SMEM] * 3 + [ANY] * 3,
            micros,
            limit,
            [
                pltpu.VMEM((steps, TILE, occ, columns), BF16),
                pltpu.VMEM((rows * occ, columns), BF16),
                pltpu.VMEM((2, rows, occ, wide // 2), BF16),
                pltpu.VMEM((2, wide // 2, columns), outs[0].dtype),
                pltpu.VMEM((2,) + piece.shape, BF16),
                pltpu.SMEM(amplitude_tiles.shape, jnp.int32),
                pltpu.SemaphoreType.DMA((steps,)),
                pltpu.SemaphoreType.DMA((2, 2)),
                pltpu.SemaphoreType.DMA((2,)),
                pltpu.SemaphoreType.DMA(()),
            ],
            spaces,
        )(vir, tile, half, amplitude_tiles, amplitudes, cholesky_vectors)

    sent, low, high = column(
        other, (shape((wide, columns), BF16), piece, piece), (ANY,) * 3, 3.0, FULL
    )
    got = lax.ppermute(sent, "c", SWAP)
    left_low = lax.ppermute(low, "x", shift(nx, 1))
    right_high = lax.ppermute(high, "x", shift(nx, -1))
    (kept,) = column(mine, (shape((wide, columns), F32),), (VMEM,), 2.0, 16)

    group = ny * nx
    chunk = wide // group
    added = call(add_kernel, shape((wide, columns), BF16), [VMEM] * 2, 0.7, 8)(kept, got)
    plane = [[group - 1 - i for i in range(group)]]
    line = [[(i + nz // 2) % nz for i in range(nz)]]

    def exchange(parts, axes, members):
        return lax.all_to_all(parts, axes, 0, 0, axis_index_groups=members, tiled=True)

    s1 = exchange(added.reshape(group, chunk, columns), ("y", "x"), plane)

    places = (0, nx - 1, 1, 2)
    w_mine, w_swap = call(
        functools.partial(w_kernel, places),
        (shape((rows, nx * rows), BF16),) * 2,
        [SMEM] * 4 + [VMEM, ANY],
        1.9,
        FULL,
    )(vir, x, mine, integral_tiles, ladder_integrals, added)
    w_other = lax.ppermute(w_swap, "c", SWAP)

    pair = shape((2,) + piece.shape, BF16)
    to_right, to_left = call(
        pieces_kernel,
        (pair, pair),
        [ANY] * 5,
        1.5,
        FULL,
        [pltpu.VMEM((4,) + piece.shape, BF16), pltpu.SemaphoreType.DMA((2, 4))],
        (ANY,) * 2,
    )(low, high, left_low, right_high, w_swap)
    from_left = lax.ppermute(to_right, "x", shift(nx, 1))
    from_right = lax.ppermute(to_left, "x", shift(nx, -1))

    def summed(receivers, *parts):
        return call(
            sum_kernel,
            shape((receivers, chunk, columns), BF16),
            [VMEM] * len(parts),
            1.0,
            8,
        )(*parts)

    s2 = exchange(summed(nz, s1), "z", line)
    third = summed(group, s2)
    s3 = exchange(third, ("y", "x"), plane)

    half_out = shape((rows * occ // 2, columns), BF16)
    base, low_sent, high_sent = call(
        ladder_kernel,
        (shape((rows * occ, columns), BF16), half_out, half_out),
        [ANY] * 10,
        5.0,
        FULL,
        [
            pltpu.VMEM((occ, nx * rows, columns), BF16),
            pltpu.VMEM((2 * rows, nx * rows), BF16),
            pltpu.VMEM((rows, occ, columns), BF16),
            pltpu.VMEM((steps, TILE * occ, columns), BF16),
            pltpu.VMEM((steps, TILE * occ, columns), BF16),
            pltpu.SemaphoreType.DMA((9, occ)),
            pltpu.SemaphoreType.DMA((2 * steps,)),
        ],
        (ANY, ANY, ANY),
    )(
        w_mine, w_other, source_block, low, high, left_low, right_high, from_left, from_right, third
    )
    low_got = lax.ppermute(low_sent, "c", SWAP)
    high_got = lax.ppermute(high_sent, "c", SWAP)
    ct_mine = s3.reshape(wide, columns)
    ct_other = lax.ppermute(ct_mine, "c", SWAP)
    first = call(
        first_kernel, shape((rows * occ, columns), F32), [SMEM] + [VMEM] * 3, 0.9, 12
    )(mine, cholesky_vectors, ct_mine, base)
    return call(
        last_kernel,
        shape((rows, occ, columns), BF16),
        [SMEM] + [VMEM] * 5,
        2.0,
        16,
        [
            pltpu.VMEM((steps, TILE, occ, columns), BF16),
            pltpu.SemaphoreType.DMA((steps,)),
        ],
        ANY,
    )(other, cholesky_vectors, ct_other, first, low_got, high_got)


def solution(mesh):
    split = Mesh(mesh.devices.reshape(4, 8, 4, 2), ("y", "z", "x", "c"))
    rows, cols = ("x", "c"), ("y", "z")
    return jax.shard_map(
        shards,
        mesh=split,
        in_specs=(
            P(rows, cols, None),
            P(rows, cols, None),
            P(rows, None),
            P(rows, cols, None),
            P(),
            P(),
        ),
        out_specs=P(rows, cols, None),
        check_vma=False,
    )
```

```python
import functools

import jax
import jax.numpy as jnp
from jax import lax
from jax.experimental import pallas as pl
from jax.experimental.pallas import tpu as pltpu
from jax.sharding import Mesh, PartitionSpec as P

TILE = 64
FULL = 58
SWAP = [(0, 1), (1, 0)]
F32, BF16 = jnp.float32, jnp.bfloat16
VMEM = pl.BlockSpec(memory_space=pltpu.VMEM)
SMEM = pl.BlockSpec(memory_space=pltpu.SMEM)
ANY = pl.BlockSpec(memory_space=pl.ANY)
shape = jax.ShapeDtypeStruct


def shift(n, d):
    return [(i, (i + d) % n) for i in range(n)]


def call(kernel, outs, specs, micros, limit, scratch=(), spaces=None, grid=()):
    return pl.pallas_call(
        kernel,
        out_shape=outs,
        grid=grid,
        in_specs=specs,
        out_specs=spaces or jax.tree.map(lambda _: VMEM, outs),
        scratch_shapes=scratch,
        compiler_params=pltpu.CompilerParams(vmem_limit_bytes=limit * 2**20),
        cost_estimate=pl.CostEstimate(
            flops=0, bytes_accessed=int(micros * 3.4e6), transcendentals=0
        ),
    )


def dot(a, b, over=1):
    return lax.dot_general(a, b, (((over,), (0,)), ((), ())), preferred_element_type=F32)


def permutation(n, occ):
    row = lax.broadcasted_iota(jnp.int32, (n, n), 0)
    col = lax.broadcasted_iota(jnp.int32, (n, n), 1)
    per = n // occ
    return jnp.where(col == (row % per) * occ + row // per, 1.0, 0.0).astype(BF16)


def column_kernel(vir, tile, half, tiles, t, chol, out, *refs):
    pieces = refs[:-10]
    t_buf, masked, chol_buf, out_buf, laid, mask, t_sems, sems, piece_sems, mask_sem = refs[-10:]
    rows, occ, cols = t.shape
    parts, width = out_buf.shape[:2]
    steps = rows // TILE
    group = TILE * occ
    start = pl.multiple_of(half[0] * parts * width, parts * width)
    mask_copy = pltpu.make_async_copy(tiles, mask, mask_sem)
    t_copies = [
        pltpu.make_async_copy(t.at[pl.ds(v * TILE, TILE)], t_buf.at[v], t_sems.at[v])
        for v in range(steps)
    ]
    chol_copies = [
        pltpu.make_async_copy(
            chol.at[:, :, pl.ds(start + i * width, width)], chol_buf.at[i], sems.at[0, i]
        )
        for i in range(parts)
    ]
    for copy in [mask_copy] + t_copies + chol_copies:
        copy.start()
    k_id = lax.broadcasted_iota(jnp.int32, (occ, cols), 0)
    perm = permutation(group, occ)
    outgoing = []
    mask_copy.wait()
    for v in range(steps):
        keep = jnp.zeros((occ, cols), F32)
        for k in range(occ):
            kept = mask[vir[0] * steps + v, tile[0] * occ + k]
            keep = jnp.where(k_id == k, kept.astype(F32), keep)
        t_copies[v].wait()
        here = (t_buf[v] * keep.astype(BF16)[None]).reshape(group, cols)
        masked[v * group:(v + 1) * group] = here
        if pieces:
            moved = dot(perm, here).astype(BF16)
            which, place = divmod(v, steps // 2)
            for k in range(occ):
                laid[which, k, place * TILE:(place + 1) * TILE] = moved[k * TILE:(k + 1) * TILE]
            if place == steps // 2 - 1:
                outgoing.append(
                    pltpu.make_async_copy(laid.at[which], pieces[which], piece_sems.at[which])
                )
                outgoing[-1].start()
    for i in range(parts):
        chol_copies[i].wait()
        left = chol_buf[i].reshape(rows * occ, width)
        out_buf[i] = dot(left, masked[...], 0).astype(out_buf.dtype)
        outgoing.append(
            pltpu.make_async_copy(out_buf.at[i], out.at[pl.ds(i * width, width)], sems.at[1, i])
        )
        outgoing[-1].start()
    for copy in outgoing:
        copy.wait()


def add_kernel(kept, got, out):
    out[...] = (kept[...] + got[...].astype(F32)).astype(BF16)


def w_kernel(places, vir, x, core, tiles, w, after, mine, other):
    rows = w.shape[0]
    steps = rows // TILE
    ring = len(places)
    lane = lax.broadcasted_iota(jnp.int32, (TILE, 2 * TILE), 1)
    for i, d in enumerate(places):
        for out, which in ((mine, core[0]), (other, 1 - core[0])):
            block = ((x[0] + d) % ring) * 2 + which
            for j in range(rows // (2 * TILE)):
                at = pl.ds(pl.multiple_of(block * rows + j * 2 * TILE, 2 * TILE), 2 * TILE)
                col = block * steps + 2 * j
                for v in range(steps):
                    row = vir[0] * steps + v
                    keep = jnp.where(
                        lane < TILE, tiles[row, col].astype(F32), tiles[row, col + 1].astype(F32)
                    )
                    here = slice(v * TILE, (v + 1) * TILE)
                    to = slice(i * rows + j * 2 * TILE, i * rows + (j + 1) * 2 * TILE)
                    out[here, to] = w[here, at] * keep.astype(BF16)


def pieces_kernel(low, high, left, right, after, to_right, to_left, held, sems):
    pairs = (
        (high, to_right.at[0]), (low, to_left.at[0]), (left, to_right.at[1]), (right, to_left.at[1])
    )
    inward = [
        pltpu.make_async_copy(source, held.at[i], sems.at[0, i])
        for i, (source, _) in enumerate(pairs)
    ]
    outward = [
        pltpu.make_async_copy(held.at[i], out, sems.at[1, i]) for i, (_, out) in enumerate(pairs)
    ]
    for copy in inward:
        copy.start()
    for copy, then in zip(inward, outward):
        copy.wait()
        then.start()
    for copy in outward:
        copy.wait()


def sum_kernel(parts, *refs):
    out = refs[-1]
    total = parts[0].astype(F32)
    for i in range(1, parts.shape[0]):
        total = total + parts[i].astype(F32)
    total = total.astype(BF16)
    for i in range(out.shape[0]):
        out[i] = total


def ladder_kernel(
    w_mine, w_other, source, low, high, left_low, right_high, from_left, from_right, after,
    base, low_sent, high_sent, right, w_held, source_held, base_held, sent_held, in_sems, out_sems,
):
    rows, occ, cols = source.shape
    pieces = (
        low, high, left_low, from_left.at[0], from_right.at[0], right_high, from_left.at[1],
        from_right.at[1],
    )
    steps = rows // TILE
    group = TILE * occ
    size = pieces[0].shape[1]
    w_copies = [
        pltpu.make_async_copy(w_other, w_held.at[pl.ds(0, rows)], in_sems.at[len(pieces), 0]),
        pltpu.make_async_copy(w_mine, w_held.at[pl.ds(rows, rows)], in_sems.at[len(pieces), 1]),
    ]
    source_copy = pltpu.make_async_copy(source, source_held, in_sems.at[len(pieces), 2])
    copies = [
        [
            pltpu.make_async_copy(
                piece.at[k], right.at[k, pl.ds(i * size, size)], in_sems.at[i, k]
            )
            for i, piece in enumerate(pieces)
        ]
        for k in range(occ)
    ]
    for copy in w_copies + sum(copies, []) + [source_copy]:
        copy.start()
    back = permutation(group, occ)
    for copy in w_copies:
        copy.wait()
    w = w_held[...]
    sums = []
    for k in range(occ):
        for copy in copies[k]:
            copy.wait()
        sums.append(dot(w, right[k]).astype(BF16))
    source_copy.wait()
    outward = []
    for v in range(2 * steps):
        here = slice(v * TILE, (v + 1) * TILE)
        own = dot(back, jnp.concatenate([part[here] for part in sums], 0), 0)
        if v < steps:
            sent_held[v] = own.astype(BF16)
            from_, to = sent_held.at[v], (low_sent, high_sent)[v * 2 // steps]
            at = pl.ds((v % (steps // 2)) * group, group)
        else:
            mine = v - steps
            block = source_held[mine * TILE:(mine + 1) * TILE].reshape(group, cols)
            base_held[mine] = (own + block.astype(F32)).astype(BF16)
            from_, to, at = base_held.at[mine], base, pl.ds(mine * group, group)
        outward.append(pltpu.make_async_copy(from_, to.at[at], out_sems.at[v]))
        outward[-1].start()
    for copy in outward:
        copy.wait()


def first_kernel(half, chol, ct, base, out):
    rows, occ, _ = chol.shape
    width = ct.shape[0]
    start = pl.multiple_of(half[0] * width, width)
    total = dot(chol[:, :, pl.ds(start, width)].reshape(rows * occ, width), ct[...])
    out[...] = total + base[...].astype(F32)


def last_kernel(half, chol, ct, first, got_low, got_high, out, held, sems):
    rows, occ, _ = chol.shape
    width = ct.shape[0]
    steps = held.shape[0]
    each = rows // steps
    group = each * occ
    start = pl.multiple_of(half[0] * width, width)
    copies = []
    for v in range(steps):
        here = slice(v * each, (v + 1) * each)
        total = dot(chol[here, :, pl.ds(start, width)].reshape(group, width), ct[...])
        got = (got_low, got_high)[v * 2 // steps]
        at = (v % (steps // 2)) * group
        part = first[v * group:(v + 1) * group] + got[at:at + group].astype(F32)
        held[v] = (total + part).astype(BF16).reshape(held.shape[1:])
        copies.append(
            pltpu.make_async_copy(held.at[v], out.at[pl.ds(v * each, each)], sems.at[v])
        )
        copies[-1].start()
    for copy in copies:
        copy.wait()


def shards(
    amplitudes, source_block, ladder_integrals, cholesky_vectors, integral_tiles, amplitude_tiles
):
    rows, occ, columns = amplitudes.shape
    vectors = cholesky_vectors.shape[2]
    wide = vectors // 2
    steps = rows // TILE
    ny, nz, nx = lax.axis_size("y"), lax.axis_size("z"), lax.axis_size("x")
    core, x = lax.axis_index("c"), lax.axis_index("x")
    tile = lax.axis_index("y") * nz + lax.axis_index("z")
    vir = (x * 2 + core)[None]
    tile, x, mine, other = tile[None], x[None], core[None], 1 - core[None]

    row_half = rows // 2
    piece = shape((occ, row_half, columns), BF16)

    def column(half, outs, spaces, micros, limit):
        return call(
            column_kernel,
            outs,
            [SMEM] * 3 + [ANY] * 3,
            micros,
            limit,
            [
                pltpu.VMEM((steps, TILE, occ, columns), BF16),
                pltpu.VMEM((rows * occ, columns), BF16),
                pltpu.VMEM((2, rows, occ, wide // 2), BF16),
                pltpu.VMEM((2, wide // 2, columns), outs[0].dtype),
                pltpu.VMEM((2,) + piece.shape, BF16),
                pltpu.SMEM(amplitude_tiles.shape, jnp.int32),
                pltpu.SemaphoreType.DMA((steps,)),
                pltpu.SemaphoreType.DMA((2, 2)),
                pltpu.SemaphoreType.DMA((2,)),
                pltpu.SemaphoreType.DMA(()),
            ],
            spaces,
        )(vir, tile, half, amplitude_tiles, amplitudes, cholesky_vectors)

    sent, low, high = column(
        other, (shape((wide, columns), BF16), piece, piece), (ANY,) * 3, 3.0, FULL
    )
    got = lax.ppermute(sent, "c", SWAP)
    left_low = lax.ppermute(low, "x", shift(nx, 1))
    right_high = lax.ppermute(high, "x", shift(nx, -1))
    (kept,) = column(mine, (shape((wide, columns), F32),), (VMEM,), 2.0, 16)

    group = ny * nx
    chunk = wide // group
    added = call(add_kernel, shape((wide, columns), BF16), [VMEM] * 2, 0.7, 8)(kept, got)
    plane = [[row * nx + col for row in range(ny) for col in reversed(range(nx))]]
    line = [[(i + nz // 2) % nz for i in range(nz)]]

    def exchange(parts, axes, members):
        return lax.all_to_all(parts, axes, 0, 0, axis_index_groups=members, tiled=True)

    s1 = exchange(added.reshape(group, chunk, columns), ("y", "x"), plane)

    places = (0, nx - 1, 1, 2)
    w_mine, w_swap = call(
        functools.partial(w_kernel, places),
        (shape((rows, nx * rows), BF16),) * 2,
        [SMEM] * 4 + [VMEM, ANY],
        1.9,
        FULL,
    )(vir, x, mine, integral_tiles, ladder_integrals, added)
    w_other = lax.ppermute(w_swap, "c", SWAP)

    pair = shape((2,) + piece.shape, BF16)
    to_right, to_left = call(
        pieces_kernel,
        (pair, pair),
        [ANY] * 5,
        1.5,
        FULL,
        [pltpu.VMEM((4,) + piece.shape, BF16), pltpu.SemaphoreType.DMA((2, 4))],
        (ANY,) * 2,
    )(low, high, left_low, right_high, w_swap)
    from_left = lax.ppermute(to_right, "x", shift(nx, 1))
    from_right = lax.ppermute(to_left, "x", shift(nx, -1))

    def summed(receivers, *parts):
        return call(
            sum_kernel,
            shape((receivers, chunk, columns), BF16),
            [VMEM] * len(parts),
            1.0,
            8,
        )(*parts)

    s2 = exchange(summed(nz, s1), "z", line)
    third = summed(group, s2)
    s3 = exchange(third, ("y", "x"), plane)

    half_out = shape((rows * occ // 2, columns), BF16)
    base, low_sent, high_sent = call(
        ladder_kernel,
        (shape((rows * occ, columns), BF16), half_out, half_out),
        [ANY] * 10,
        5.0,
        FULL,
        [
            pltpu.VMEM((occ, nx * rows, columns), BF16),
            pltpu.VMEM((2 * rows, nx * rows), BF16),
            pltpu.VMEM((rows, occ, columns), BF16),
            pltpu.VMEM((steps, TILE * occ, columns), BF16),
            pltpu.VMEM((steps, TILE * occ, columns), BF16),
            pltpu.SemaphoreType.DMA((9, occ)),
            pltpu.SemaphoreType.DMA((2 * steps,)),
        ],
        (ANY, ANY, ANY),
    )(
        w_mine, w_other, source_block, low, high, left_low, right_high, from_left, from_right, third
    )
    low_got = lax.ppermute(low_sent, "c", SWAP)
    high_got = lax.ppermute(high_sent, "c", SWAP)
    ct_mine = s3.reshape(wide, columns)
    ct_other = lax.ppermute(ct_mine, "c", SWAP)
    first = call(
        first_kernel, shape((rows * occ, columns), F32), [SMEM] + [VMEM] * 3, 0.9, 12
    )(mine, cholesky_vectors, ct_mine, base)
    return call(
        last_kernel,
        shape((rows, occ, columns), BF16),
        [SMEM] + [VMEM] * 5,
        2.0,
        16,
        [
            pltpu.VMEM((steps, TILE, occ, columns), BF16),
            pltpu.SemaphoreType.DMA((steps,)),
        ],
        ANY,
    )(other, cholesky_vectors, ct_other, first, low_got, high_got)


def solution(mesh):
    split = Mesh(mesh.devices.reshape(4, 8, 4, 2), ("y", "z", "x", "c"))
    rows, cols = ("x", "c"), ("y", "z")
    return jax.shard_map(
        shards,
        mesh=split,
        in_specs=(
            P(rows, cols, None),
            P(rows, cols, None),
            P(rows, None),
            P(rows, cols, None),
            P(),
            P(),
        ),
        out_specs=P(rows, cols, None),
        check_vma=False,
    )
```

```python
import functools

import jax
import jax.numpy as jnp
from jax import lax
from jax.experimental import pallas as pl
from jax.experimental.pallas import tpu as pltpu
from jax.sharding import Mesh, PartitionSpec as P

TILE = 64
FULL = 58
SWAP = [(0, 1), (1, 0)]
F32, BF16 = jnp.float32, jnp.bfloat16
VMEM = pl.BlockSpec(memory_space=pltpu.VMEM)
SMEM = pl.BlockSpec(memory_space=pltpu.SMEM)
ANY = pl.BlockSpec(memory_space=pl.ANY)
shape = jax.ShapeDtypeStruct


def shift(n, d):
    return [(i, (i + d) % n) for i in range(n)]


def call(kernel, outs, specs, micros, limit, scratch=(), spaces=None, grid=()):
    return pl.pallas_call(
        kernel,
        out_shape=outs,
        grid=grid,
        in_specs=specs,
        out_specs=spaces or jax.tree.map(lambda _: VMEM, outs),
        scratch_shapes=scratch,
        compiler_params=pltpu.CompilerParams(vmem_limit_bytes=limit * 2**20),
        cost_estimate=pl.CostEstimate(
            flops=0, bytes_accessed=int(micros * 3.4e6), transcendentals=0
        ),
    )


def dot(a, b, over=1):
    return lax.dot_general(a, b, (((over,), (0,)), ((), ())), preferred_element_type=F32)


def permutation(n, occ):
    row = lax.broadcasted_iota(jnp.int32, (n, n), 0)
    col = lax.broadcasted_iota(jnp.int32, (n, n), 1)
    per = n // occ
    return jnp.where(col == (row % per) * occ + row // per, 1.0, 0.0).astype(BF16)


def column_kernel(vir, tile, half, tiles, t, chol, out, *refs):
    pieces = refs[:-10]
    t_buf, masked, chol_buf, out_buf, laid, mask, t_sems, sems, piece_sems, mask_sem = refs[-10:]
    rows, occ, cols = t.shape
    parts, width = out_buf.shape[:2]
    steps = rows // TILE
    group = TILE * occ
    start = pl.multiple_of(half[0] * parts * width, parts * width)
    mask_copy = pltpu.make_async_copy(tiles, mask, mask_sem)
    t_copies = [
        pltpu.make_async_copy(t.at[pl.ds(v * TILE, TILE)], t_buf.at[v], t_sems.at[v])
        for v in range(steps)
    ]
    chol_copies = [
        pltpu.make_async_copy(
            chol.at[:, :, pl.ds(start + i * width, width)], chol_buf.at[i], sems.at[0, i]
        )
        for i in range(parts)
    ]
    for copy in [mask_copy] + t_copies + chol_copies:
        copy.start()
    k_id = lax.broadcasted_iota(jnp.int32, (occ, cols), 0)
    perm = permutation(group, occ)
    outgoing = []
    mask_copy.wait()
    for v in range(steps):
        keep = jnp.zeros((occ, cols), F32)
        for k in range(occ):
            kept = mask[vir[0] * steps + v, tile[0] * occ + k]
            keep = jnp.where(k_id == k, kept.astype(F32), keep)
        t_copies[v].wait()
        here = (t_buf[v] * keep.astype(BF16)[None]).reshape(group, cols)
        masked[v * group:(v + 1) * group] = here
        if pieces:
            moved = dot(perm, here).astype(BF16)
            which, place = divmod(v, steps // 2)
            for k in range(occ):
                laid[which, k, place * TILE:(place + 1) * TILE] = moved[k * TILE:(k + 1) * TILE]
            if place == steps // 2 - 1:
                outgoing.append(
                    pltpu.make_async_copy(laid.at[which], pieces[which], piece_sems.at[which])
                )
                outgoing[-1].start()
    for i in range(parts):
        chol_copies[i].wait()
        left = chol_buf[i].reshape(rows * occ, width)
        out_buf[i] = dot(left, masked[...], 0).astype(out_buf.dtype)
        outgoing.append(
            pltpu.make_async_copy(out_buf.at[i], out.at[pl.ds(i * width, width)], sems.at[1, i])
        )
        outgoing[-1].start()
    for copy in outgoing:
        copy.wait()


def kept_kernel(vir, tile, half, mask, t, chol, got, out):
    rows, occ, cols = t.shape
    width = out.shape[0]
    steps = rows // TILE
    start = pl.multiple_of(half[0] * width, width)
    k_id = lax.broadcasted_iota(jnp.int32, (occ, cols), 0)
    parts = []
    for v in range(steps):
        keep = jnp.zeros((occ, cols), F32)
        for k in range(occ):
            kept = mask[vir[0] * steps + v, tile[0] * occ + k]
            keep = jnp.where(k_id == k, kept.astype(F32), keep)
        parts.append(t[v * TILE:(v + 1) * TILE] * keep.astype(BF16)[None])
    masked = jnp.concatenate(parts, 0).reshape(rows * occ, cols)
    left = chol[:, :, pl.ds(start, width)].reshape(rows * occ, width)
    out[...] = (dot(left, masked, 0) + got[...].astype(F32)).astype(BF16)


def w_kernel(places, vir, x, core, tiles, w, after, mine, other):
    rows = w.shape[0]
    steps = rows // TILE
    ring = len(places)
    lane = lax.broadcasted_iota(jnp.int32, (TILE, 2 * TILE), 1)
    for i, d in enumerate(places):
        for out, which in ((mine, core[0]), (other, 1 - core[0])):
            block = ((x[0] + d) % ring) * 2 + which
            for j in range(rows // (2 * TILE)):
                at = pl.ds(pl.multiple_of(block * rows + j * 2 * TILE, 2 * TILE), 2 * TILE)
                col = block * steps + 2 * j
                for v in range(steps):
                    row = vir[0] * steps + v
                    keep = jnp.where(
                        lane < TILE, tiles[row, col].astype(F32), tiles[row, col + 1].astype(F32)
                    )
                    here = slice(v * TILE, (v + 1) * TILE)
                    to = slice(i * rows + j * 2 * TILE, i * rows + (j + 1) * 2 * TILE)
                    out[here, to] = w[here, at] * keep.astype(BF16)


def pieces_kernel(low, high, left, right, after, to_right, to_left, held, sems):
    pairs = (
        (high, to_right.at[0]), (low, to_left.at[0]), (left, to_right.at[1]), (right, to_left.at[1])
    )
    inward = [
        pltpu.make_async_copy(source, held.at[i], sems.at[0, i])
        for i, (source, _) in enumerate(pairs)
    ]
    outward = [
        pltpu.make_async_copy(held.at[i], out, sems.at[1, i]) for i, (_, out) in enumerate(pairs)
    ]
    for copy in inward:
        copy.start()
    for copy, then in zip(inward, outward):
        copy.wait()
        then.start()
    for copy in outward:
        copy.wait()


def sum_kernel(parts, *refs):
    out = refs[-1]
    total = parts[0].astype(F32)
    for i in range(1, parts.shape[0]):
        total = total + parts[i].astype(F32)
    total = total.astype(BF16)
    for i in range(out.shape[0]):
        out[i] = total


def ladder_kernel(
    w_mine, w_other, source, low, high, left_low, right_high, from_left, from_right, after,
    base, low_sent, high_sent, right, w_held, source_held, base_held, sent_held, in_sems, out_sems,
):
    rows, occ, cols = source.shape
    pieces = (
        low, high, left_low, from_left.at[0], from_right.at[0], right_high, from_left.at[1],
        from_right.at[1],
    )
    steps = rows // TILE
    group = TILE * occ
    size = pieces[0].shape[1]
    w_copies = [
        pltpu.make_async_copy(w_other, w_held.at[pl.ds(0, rows)], in_sems.at[len(pieces), 0]),
        pltpu.make_async_copy(w_mine, w_held.at[pl.ds(rows, rows)], in_sems.at[len(pieces), 1]),
    ]
    source_copy = pltpu.make_async_copy(source, source_held, in_sems.at[len(pieces), 2])
    copies = [
        [
            pltpu.make_async_copy(
                piece.at[k], right.at[k, pl.ds(i * size, size)], in_sems.at[i, k]
            )
            for i, piece in enumerate(pieces)
        ]
        for k in range(occ)
    ]
    for copy in w_copies + sum(copies, []) + [source_copy]:
        copy.start()
    back = permutation(group, occ)
    for copy in w_copies:
        copy.wait()
    w = w_held[...]
    sums = []
    for k in range(occ):
        for copy in copies[k]:
            copy.wait()
        sums.append(dot(w, right[k]).astype(BF16))
    source_copy.wait()
    outward = []
    for v in range(2 * steps):
        here = slice(v * TILE, (v + 1) * TILE)
        own = dot(back, jnp.concatenate([part[here] for part in sums], 0), 0)
        if v < steps:
            sent_held[v] = own.astype(BF16)
            from_, to = sent_held.at[v], (low_sent, high_sent)[v * 2 // steps]
            at = pl.ds((v % (steps // 2)) * group, group)
        else:
            mine = v - steps
            block = source_held[mine * TILE:(mine + 1) * TILE].reshape(group, cols)
            base_held[mine] = (own + block.astype(F32)).astype(BF16)
            from_, to, at = base_held.at[mine], base, pl.ds(mine * group, group)
        outward.append(pltpu.make_async_copy(from_, to.at[at], out_sems.at[v]))
        outward[-1].start()
    for copy in outward:
        copy.wait()


def first_kernel(half, chol, ct, base, out):
    rows, occ, _ = chol.shape
    width = ct.shape[0]
    start = pl.multiple_of(half[0] * width, width)
    total = dot(chol[:, :, pl.ds(start, width)].reshape(rows * occ, width), ct[...])
    out[...] = total + base[...].astype(F32)


def last_kernel(half, chol, ct, first, got_low, got_high, out, held, sems):
    rows, occ, _ = chol.shape
    width = ct.shape[0]
    steps = held.shape[0]
    each = rows // steps
    group = each * occ
    start = pl.multiple_of(half[0] * width, width)
    copies = []
    for v in range(steps):
        here = slice(v * each, (v + 1) * each)
        total = dot(chol[here, :, pl.ds(start, width)].reshape(group, width), ct[...])
        got = (got_low, got_high)[v * 2 // steps]
        at = (v % (steps // 2)) * group
        part = first[v * group:(v + 1) * group] + got[at:at + group].astype(F32)
        held[v] = (total + part).astype(BF16).reshape(held.shape[1:])
        copies.append(
            pltpu.make_async_copy(held.at[v], out.at[pl.ds(v * each, each)], sems.at[v])
        )
        copies[-1].start()
    for copy in copies:
        copy.wait()


def shards(
    amplitudes, source_block, ladder_integrals, cholesky_vectors, integral_tiles, amplitude_tiles
):
    rows, occ, columns = amplitudes.shape
    vectors = cholesky_vectors.shape[2]
    wide = vectors // 2
    steps = rows // TILE
    ny, nz, nx = lax.axis_size("y"), lax.axis_size("z"), lax.axis_size("x")
    core, x = lax.axis_index("c"), lax.axis_index("x")
    tile = lax.axis_index("y") * nz + lax.axis_index("z")
    vir = (x * 2 + core)[None]
    tile, x, mine, other = tile[None], x[None], core[None], 1 - core[None]

    row_half = rows // 2
    piece = shape((occ, row_half, columns), BF16)

    def column(half, outs, spaces, micros, limit):
        return call(
            column_kernel,
            outs,
            [SMEM] * 3 + [ANY] * 3,
            micros,
            limit,
            [
                pltpu.VMEM((steps, TILE, occ, columns), BF16),
                pltpu.VMEM((rows * occ, columns), BF16),
                pltpu.VMEM((2, rows, occ, wide // 2), BF16),
                pltpu.VMEM((2, wide // 2, columns), outs[0].dtype),
                pltpu.VMEM((2,) + piece.shape, BF16),
                pltpu.SMEM(amplitude_tiles.shape, jnp.int32),
                pltpu.SemaphoreType.DMA((steps,)),
                pltpu.SemaphoreType.DMA((2, 2)),
                pltpu.SemaphoreType.DMA((2,)),
                pltpu.SemaphoreType.DMA(()),
            ],
            spaces,
        )(vir, tile, half, amplitude_tiles, amplitudes, cholesky_vectors)

    sent, low, high = column(
        other, (shape((wide, columns), BF16), piece, piece), (ANY,) * 3, 3.0, FULL
    )
    got = lax.ppermute(sent, "c", SWAP)
    left_low = lax.ppermute(low, "x", shift(nx, 1))
    right_high = lax.ppermute(high, "x", shift(nx, -1))
    group = ny * nx
    chunk = wide // group
    added = call(
        kept_kernel, shape((wide, columns), BF16), [SMEM] * 4 + [VMEM] * 3, 2.2, 16
    )(vir, tile, mine, amplitude_tiles, amplitudes, cholesky_vectors, got)
    plane = [[row * nx + col for row in range(ny) for col in reversed(range(nx))]]
    line = [[(i + nz // 2) % nz for i in range(nz)]]

    def exchange(parts, axes, members):
        return lax.all_to_all(parts, axes, 0, 0, axis_index_groups=members, tiled=True)

    s1 = exchange(added.reshape(group, chunk, columns), ("y", "x"), plane)

    places = (0, nx - 1, 1, 2)
    w_mine, w_swap = call(
        functools.partial(w_kernel, places),
        (shape((rows, nx * rows), BF16),) * 2,
        [SMEM] * 4 + [VMEM, ANY],
        1.9,
        FULL,
    )(vir, x, mine, integral_tiles, ladder_integrals, added)
    w_other = lax.ppermute(w_swap, "c", SWAP)

    pair = shape((2,) + piece.shape, BF16)
    to_right, to_left = call(
        pieces_kernel,
        (pair, pair),
        [ANY] * 5,
        1.5,
        FULL,
        [pltpu.VMEM((4,) + piece.shape, BF16), pltpu.SemaphoreType.DMA((2, 4))],
        (ANY,) * 2,
    )(low, high, left_low, right_high, w_swap)
    from_left = lax.ppermute(to_right, "x", shift(nx, 1))
    from_right = lax.ppermute(to_left, "x", shift(nx, -1))

    def summed(receivers, *parts):
        return call(
            sum_kernel,
            shape((receivers, chunk, columns), BF16),
            [VMEM] * len(parts),
            1.0,
            8,
        )(*parts)

    s2 = exchange(summed(nz, s1), "z", line)
    third = summed(group, s2)
    s3 = exchange(third, ("y", "x"), plane)

    half_out = shape((rows * occ // 2, columns), BF16)
    base, low_sent, high_sent = call(
        ladder_kernel,
        (shape((rows * occ, columns), BF16), half_out, half_out),
        [ANY] * 10,
        5.0,
        FULL,
        [
            pltpu.VMEM((occ, nx * rows, columns), BF16),
            pltpu.VMEM((2 * rows, nx * rows), BF16),
            pltpu.VMEM((rows, occ, columns), BF16),
            pltpu.VMEM((steps, TILE * occ, columns), BF16),
            pltpu.VMEM((steps, TILE * occ, columns), BF16),
            pltpu.SemaphoreType.DMA((9, occ)),
            pltpu.SemaphoreType.DMA((2 * steps,)),
        ],
        (ANY, ANY, ANY),
    )(
        w_mine, w_other, source_block, low, high, left_low, right_high, from_left, from_right, third
    )
    low_got = lax.ppermute(low_sent, "c", SWAP)
    high_got = lax.ppermute(high_sent, "c", SWAP)
    ct_mine = s3.reshape(wide, columns)
    ct_other = lax.ppermute(ct_mine, "c", SWAP)
    first = call(
        first_kernel, shape((rows * occ, columns), F32), [SMEM] + [VMEM] * 3, 0.9, 12
    )(mine, cholesky_vectors, ct_mine, base)
    return call(
        last_kernel,
        shape((rows, occ, columns), BF16),
        [SMEM] + [VMEM] * 5,
        2.0,
        16,
        [
            pltpu.VMEM((steps, TILE, occ, columns), BF16),
            pltpu.SemaphoreType.DMA((steps,)),
        ],
        ANY,
    )(other, cholesky_vectors, ct_other, first, low_got, high_got)


def solution(mesh):
    split = Mesh(mesh.devices.reshape(4, 8, 4, 2), ("y", "z", "x", "c"))
    rows, cols = ("x", "c"), ("y", "z")
    return jax.shard_map(
        shards,
        mesh=split,
        in_specs=(
            P(rows, cols, None),
            P(rows, cols, None),
            P(rows, None),
            P(rows, cols, None),
            P(),
            P(),
        ),
        out_specs=P(rows, cols, None),
        check_vma=False,
    )
```
